512 devices in a mesh: grp: 16 (over z, core), ang: 32 (over x, y).
Axes of the slice: x: 4, y: 8, z: 8, core: 2. Of those that a mesh axis runs over, the one named last changes fastest.
Arguments:
- slab_views: bfloat16 [16, 32, 1024, 1024], P('grp', None, 'ang'), may hold values from -6 to 6
- footprint: int32 [16, 32, 8], P('grp'), may hold values from -1 to 31, as said below
- row_shift: float32 [16, 32], P('grp'), may hold values from 0 to 16
- stretch: float32 [16, 32], P('grp'), may hold values from 0.8 to 0.95
- projections: bfloat16 [32, 2, 2048, 1024], P('ang', None, 'grp'), may hold values from -6 to 6
Outputs:
- row_grad: bfloat16 [32, 2, 2048, 1024], P('ang', None, 'grp')
- filter_grad: float32 [2, 16, 512], P(None, 'grp')
The draws below stay inside these ranges and needn't reach their ends.
Inputs may be any that keep to these rules, and one draw needn't show every extreme that they name: `footprint`: each list starts with 4 to 8 consecutive tile numbers and is padded with -1 after them; in every draw one list is full and ends at the last tile.
All inputs are finite; a program needn't handle non-finite values.
Results may differ from the reference program's by a relative error of at most 0.0065.
Values may be sent and summed in bfloat16 or wider, within the bound.
No kernel may reach another device: no remote copies, remote signals or barrier semaphores. Data moves between devices by JAX's collectives and lax.ppermute only.
A program may use at most 128 MiB of HBM per device.

```python
import math
import jax
import jax.numpy as jnp
from jax import lax

W = 1024
TR = 128
KF = 8
SZ = 1024
TPO = 2
SLABS = 16
ANGLES = 32
CYCLE = 2048
N_GRP = 16


def draw_footprint(key, part):
    key = jax.random.fold_in(key, 7)
    key_count, key_first, key_full = jax.random.split(key, 3)
    tiles_total = TPO * N_GRP
    counts = jax.random.randint(key_count, (N_GRP, ANGLES), KF // 2, KF + 1)
    chosen = jax.random.randint(key_full, (), 0, N_GRP * ANGLES)
    flat_index = jnp.arange(N_GRP * ANGLES).reshape(N_GRP, ANGLES)
    counts = jnp.where(flat_index == chosen, KF, counts)
    first_tile = jax.random.randint(key_first, (N_GRP, ANGLES), 0, tiles_total - counts + 1)
    first_tile = jnp.where(flat_index == chosen, tiles_total - KF, first_tile)
    entries = jnp.arange(KF)
    lists = jnp.where(entries[None, None, :] < counts[:, :, None], first_tile[:, :, None] + entries[None, None, :], -1)
    return lists.astype(jnp.int32)


def shard_levels(stream_key, shape, cuts, smallest, high):
    loudness = 1.0
    for axis_at, blocks in cuts:
        steps = jax.random.uniform(jax.random.fold_in(jax.random.fold_in(stream_key, 6), axis_at), (blocks,), jnp.float32, smallest / len(cuts), high / len(cuts))
        loudness = loudness * jnp.repeat(jnp.exp(steps), shape[axis_at] // blocks).reshape((-1,) + (1,) * (len(shape) - 1 - axis_at))
    return loudness


def normal_values(key, dims, spread, reach, cuts=(), held_as=jnp.bfloat16):
    result = jax.random.normal(key, dims, jnp.float32) * spread
    if len(cuts) > 0:
        result = shard_levels(key, dims, cuts, -0.22, 0.18) * result
    return jnp.clip(result, min=-reach, max=reach).astype(held_as)


def setup_inputs(seed: int = 0) -> dict:
    seeds = jax.random.split(jax.random.key(seed), 6)
    return {
        "slab_views": normal_values(seeds[0], (SLABS, ANGLES, W, SZ), 1.0, 6.0, ((0, 16), (2, 32))),
        "footprint": draw_footprint(jax.random.fold_in(seeds[5], 71), 0),
        "row_shift": jnp.clip(16.0 * jax.random.uniform(seeds[2], (SLABS, ANGLES), jnp.float32) ** shard_levels(seeds[2], (SLABS, ANGLES), ((0, 16),), -0.2, 0.2), 0.0, 16.0),
        "stretch": jnp.clip(0.8 + 0.14999998 * jax.random.uniform(seeds[3], (SLABS, ANGLES), jnp.float32) ** shard_levels(seeds[3], (SLABS, ANGLES), ((0, 16),), -0.2, 0.2), 0.8, 0.95),
        "projections": normal_values(seeds[4], (ANGLES, TPO, CYCLE, W), 1.0, 6.0, ((0, 32), (2, 16))),
    }


def footprint_weights(counts, offsets, stretch, entries):
    magnify = (TR * counts).astype(jnp.float32) * stretch / SZ
    row_pos = jnp.arange(TR, dtype=jnp.float32)
    depth_pos = jnp.arange(SZ, dtype=jnp.float32)
    band_pos = (TR * entries).astype(jnp.float32)[:, :, None, None] + row_pos[None, None, :, None]
    voxel_pos = offsets[:, None, None, None] + magnify[:, None, None, None] * depth_pos[None, None, None, :]
    weights = jnp.maximum(1.0 - jnp.abs(band_pos - voxel_pos) / magnify[:, None, None, None], 0.0)
    live = (entries < counts[:, None])[:, :, None, None]
    return jnp.where(live, weights, 0.0).astype(jnp.bfloat16)


def dft_basis(columns):
    column_idx = jnp.arange(columns, dtype=jnp.int32)[:, None]
    freq_idx = jnp.arange(columns // 2, dtype=jnp.int32)[None, :]
    phases = ((column_idx * freq_idx) % columns).astype(jnp.float32) * (2.0 * math.pi / columns)
    return jnp.concatenate([jnp.cos(phases), jnp.sin(phases)], axis=1).astype(jnp.bfloat16)


def reference(slab_views, footprint, row_shift, stretch, projections):
    angles = footprint.shape[1]
    columns = slab_views.shape[2]
    tiles_total = TPO * N_GRP
    counts = jnp.sum((footprint >= 0).astype(jnp.int32), axis=-1)
    entries = jnp.broadcast_to(jnp.arange(KF, dtype=jnp.int32)[None, :], (angles, KF))
    angle_idx = jnp.broadcast_to(jnp.arange(angles, dtype=jnp.int32)[:, None], (angles, KF))

    def per_slab(detector, record):
        slab_view, lists, slab_counts, offsets, stretches = record
        weights = footprint_weights(slab_counts, offsets, stretches, entries)
        contrib = jnp.einsum("akrz,acz->akrc", weights.astype(jnp.float32), slab_view.astype(jnp.float32)).astype(jnp.bfloat16)
        target = jnp.where(lists >= 0, lists, tiles_total).astype(jnp.int32)
        detector = detector.at[angle_idx, target].add(contrib.astype(jnp.float32), mode="drop")
        return detector, None

    start_detector = jnp.zeros((angles, tiles_total, TR, columns), jnp.float32)
    detector, _ = lax.scan(per_slab, start_detector, (slab_views, footprint, counts, row_shift, stretch))
    row_grad = detector.reshape(angles, TPO, N_GRP * TR, columns).astype(jnp.bfloat16)
    basis = dft_basis(columns)
    n_freq = columns // 2

    def per_angle(record):
        grad_rows, proj_rows = record
        spec_grad = jnp.dot(grad_rows.reshape(-1, columns), basis, preferred_element_type=jnp.float32)
        spec_proj = jnp.dot(proj_rows.reshape(-1, columns), basis, preferred_element_type=jnp.float32)
        product = spec_grad[:, :n_freq] * spec_proj[:, :n_freq] + spec_grad[:, n_freq:] * spec_proj[:, n_freq:]
        return jnp.sum(product.reshape(TPO, N_GRP, TR, n_freq), axis=2)

    per_angle_sums = lax.map(per_angle, (row_grad, projections))
    filter_grad = jnp.sum(per_angle_sums, axis=0) * (1.0 / (columns * angles))
    return row_grad, filter_grad
```

```python
import functools
import math

import jax
import jax.numpy as jnp
import numpy as np
from jax import lax
from jax.experimental import pallas as pl
from jax.experimental.pallas import tpu as pltpu
from jax.sharding import PartitionSpec as P

TR = 128
KF = 8
SZ = 1024
TPO = 2
WINDOW = 512
PIECE = 16
GROUPS = 2
PER_SLAB = KF // 2


def dft_basis(columns):
    column_idx = np.arange(columns, dtype=np.int64)[:, None]
    freq_idx = np.arange(columns // 2, dtype=np.int64)[None, :]
    phases = ((column_idx * freq_idx) % columns).astype(np.float64) * (2.0 * math.pi / columns)
    return np.concatenate([np.cos(phases), np.sin(phases)], axis=1).astype(jnp.bfloat16)


def contrib_kernel(place, start, slope, own, other, out):
    angles = own.shape[0]
    out[...] = jnp.zeros_like(out)
    row = lax.broadcasted_iota(jnp.int32, (PIECE, TR), 1).astype(jnp.float32)
    depth = lax.broadcasted_iota(jnp.int32, (PIECE, TR), 0).astype(jnp.float32)

    def one_angle(a, carry):
        for s, views in enumerate((own, other)):
            step = row * slope[s, a] - depth
            for j in range(PER_SLAB):
                where = place[s, a * PER_SLAB + j]
                slot = where // 8
                z0 = pl.multiple_of((where % 8) * 128, 128)
                ahead = step + start[s, a * PER_SLAB + j]
                pieces = []
                for i in range(WINDOW // PIECE):
                    away = jnp.abs(ahead - float(i * PIECE))
                    pieces.append(jnp.maximum(1.0 - away, 0.0).astype(jnp.bfloat16))
                weights = jnp.concatenate(pieces, axis=0)
                tile = jnp.dot(
                    views[a, :, pl.ds(z0, WINDOW)], weights, preferred_element_type=jnp.float32
                )
                old = out[slot // 2, a, slot % 2].astype(jnp.float32)
                out[slot // 2, a, slot % 2] = (old + tile).astype(jnp.bfloat16)
        return carry

    lax.fori_loop(0, angles, one_angle, 0)


def contributions(place, start, slope, own, other, chips):
    angles, narrow, _ = own.shape
    smem = pl.BlockSpec(memory_space=pltpu.SMEM)
    vmem = pl.BlockSpec(memory_space=pltpu.VMEM)
    return pl.pallas_call(
        contrib_kernel,
        out_shape=jax.ShapeDtypeStruct((chips, angles, TPO, narrow, TR), jnp.bfloat16),
        in_specs=[smem, smem, smem, vmem, vmem],
        out_specs=vmem,
        compiler_params=pltpu.CompilerParams(vmem_limit_bytes=32 * 1024 * 1024),
        cost_estimate=pl.CostEstimate(
            flops=2 * angles * 2 * PER_SLAB * narrow * WINDOW * TR * 8,
            bytes_accessed=angles * narrow * SZ * 4 + chips * angles * TPO * narrow * TR * 2,
            transcendentals=0,
        ),
    )(place, start, slope, own, other)


def add(*terms):
    total = terms[0].astype(jnp.float32)
    for term in terms[1:]:
        total = total + term.astype(jnp.float32)
    return total.astype(jnp.bfloat16)


def body(slab_views, footprint, row_shift, stretch, projections):
    n_grp = lax.axis_size("grp")
    n_ang = lax.axis_size("ang")
    chips = n_grp // 2
    owner = lax.axis_index("grp")
    chip, core = owner // 2, owner % 2
    views = slab_views[0]
    angles = views.shape[0]
    part = angles // GROUPS

    swap = [(i, i ^ 1) for i in range(n_grp)]
    up = [(i, (i + 2) % n_grp) for i in range(n_grp)]
    down = [(i, (i - 2) % n_grp) for i in range(n_grp)]

    counts = jnp.sum((footprint[0] >= 0).astype(jnp.int32), axis=-1)
    mine = jnp.stack(
        [
            counts.astype(jnp.float32),
            footprint[0, :, 0].astype(jnp.float32),
            row_shift[0],
            stretch[0],
        ]
    )
    both = jnp.stack([mine, lax.ppermute(mine, "grp", swap)])
    count, first = both[:, 0].astype(jnp.int32), both[:, 1].astype(jnp.int32)
    magnify = (TR * count).astype(jnp.float32) * both[:, 3] / SZ
    slope = 1.0 / magnify
    entry = ((core - first) & 1)[:, :, None] + 2 * jnp.arange(PER_SLAB, dtype=jnp.int32)
    tile = first[:, :, None] + entry
    begin = ((TR * entry).astype(jnp.float32) - both[:, 2, :, None]) * slope[:, :, None]
    block = jnp.clip(jnp.floor((begin - 1.0) / 128.0).astype(jnp.int32), 0, (SZ - WINDOW) // 128)
    start = jnp.where(entry < count[:, :, None], begin - 128.0 * block.astype(jnp.float32), -1e6)
    slot = ((((tile % n_grp) // 2) - chip) % chips) * TPO + (tile // n_grp) % TPO
    place = slot * 8 + block

    parts = []
    for g in range(GROUPS):
        own = views[g * part : (g + 1) * part]
        other = lax.ppermute(own, "grp", swap)
        at = slice(g * part, (g + 1) * part)
        parts.append(
            contributions(
                place[:, at].reshape(2, -1), start[:, at].reshape(2, -1), slope[:, at], own, other, chips
            )
        )

    def ring(held, perm, order):
        moving = lax.ppermute(held[order[0]], "grp", perm)
        for at in order[1:]:
            moving = lax.ppermute(add(moving, held[at]), "grp", perm)
        return moving

    a_up = ring(parts[0], up, (4, 3, 2, 1))
    a_down = ring(parts[0], down, (5, 6, 7))
    b_up = ring(parts[1], up, (3, 2, 1))
    b_down = ring(parts[1], down, (4, 5, 6, 7))
    summed = jnp.concatenate(
        [add(parts[0][0], a_up, a_down), add(parts[1][0], b_up, b_down)], axis=0
    )

    got = lax.all_to_all(summed, "ang", split_axis=0, concat_axis=0, tiled=True)
    columns = got.shape[0] * got.shape[2]
    rows = jnp.transpose(got, (1, 3, 0, 2)).reshape(TPO * TR, columns)
    basis = jnp.asarray(dft_basis(columns))
    n_freq = columns // 2
    spec_proj = jnp.dot(projections.reshape(-1, columns), basis, preferred_element_type=jnp.float32)
    spec_grad = jnp.dot(rows, basis, preferred_element_type=jnp.float32)
    product = (
        spec_grad[:, :n_freq] * spec_proj[:, :n_freq]
        + spec_grad[:, n_freq:] * spec_proj[:, n_freq:]
    )
    share = jnp.sum(product.reshape(TPO, TR, n_freq), axis=1).reshape(-1, 128)
    shares = lax.all_to_all(
        jnp.broadcast_to(share[None], (n_ang,) + share.shape), "ang", split_axis=0, concat_axis=0, tiled=True
    )
    filter_grad = (jnp.sum(shares, axis=0) * (1.0 / (columns * angles))).reshape(TPO, 1, n_freq)
    return rows.reshape(1, TPO, TR, columns), filter_grad


def solution(mesh):
    return jax.shard_map(
        body,
        mesh=mesh,
        in_specs=(
            P("grp", None, "ang", None),
            P("grp", None, None),
            P("grp", None),
            P("grp", None),
            P("ang", None, "grp", None),
        ),
        out_specs=(P("ang", None, "grp", None), P(None, "grp", None)),
        check_vma=False,
    )
```

```python
import functools
import math

import jax
import jax.numpy as jnp
import numpy as np
from jax import lax
from jax.experimental import pallas as pl
from jax.experimental.pallas import tpu as pltpu
from jax.sharding import PartitionSpec as P

TR = 128
KF = 8
SZ = 1024
TPO = 2
WINDOW = 512
HALF = 16
BATCH = 4
UNROLL = 8
PIECE = 16


def dft_basis(columns):
    column_idx = np.arange(columns, dtype=np.int64)[:, None]
    freq_idx = np.arange(columns // 2, dtype=np.int64)[None, :]
    phases = ((column_idx * freq_idx) % columns).astype(np.float64) * (2.0 * math.pi / columns)
    return np.concatenate([np.cos(phases), np.sin(phases)], axis=1).astype(jnp.bfloat16)


def unit_kernel(hop, half, lanes, chips, here, *refs):
    out, listed = refs[-2:]
    refs = refs[:-1]
    sources = list(zip(refs[0:-1:2], refs[1:-1:2]))
    angles = out.shape[0]
    chip, core = here[0], here[1]
    reach = chips // 2 - hop
    target = lax.rem(chip + jnp.where(core == 0, reach, -reach) + chips, chips)
    owners = 2 * chips
    out[...] = refs[-2][...] if len(refs) % 2 == 0 else jnp.zeros_like(out)
    row = lax.broadcasted_iota(jnp.int32, (PIECE, TR), 1).astype(jnp.float32)
    depth = lax.broadcasted_iota(jnp.int32, (PIECE, TR), 0)
    zero = jnp.zeros((PIECE, TR), jnp.bfloat16)

    first_angle = core * HALF if half is None else (core ^ half) * HALF
    owner = [(2 * target + (core ^ lane)).astype(jnp.float32) for lane in range(lanes)]

    def entry(meta, a, lane):
        k = owner[lane] - meta[0, a]
        k = jnp.where(k < 0.0, k + owners, k)
        return jnp.where(k < 0.0, k + owners, k)

    live = []
    for s, (meta, _) in enumerate(sources):

        def note(i, found):
            a = (first_angle + i) & (2 * HALF - 1)
            for lane in range(lanes):
                listed[s, found] = i * lanes + lane
                found = found + jnp.where(entry(meta, a, lane) < meta[1, a], 1, 0)
            return found

        live.append(lax.fori_loop(0, angles, note, jnp.int32(0), unroll=UNROLL))

    def some(at, carry):
        for m in range(BATCH):
            for s, (meta, views) in enumerate(sources):
                place = at * BATCH + m
                n = listed[s, jnp.clip(place, 0, jnp.maximum(live[s] - 1, 0))]
                i, lane = n >> (lanes - 1), n & (lanes - 1)
                a = (first_angle + i) & (2 * HALF - 1)
                k = entry(meta, a, 0) if lanes == 1 else jnp.where(
                    lane == 0, entry(meta, a, 0), entry(meta, a, 1)
                )
                slope = meta[3, a]
                begin = (TR * k - meta[2, a]) * slope
                block = jnp.clip((begin - 1.0).astype(jnp.int32) >> 7, 0, (SZ - WINDOW) // 128)
                start = jnp.where(place < live[s], begin - (128 * block).astype(jnp.float32), -1e4)
                cycle = jnp.where(meta[0, a] + k >= owners, 1, 0)
                centre = row * slope + start
                below = jnp.floor(centre)
                above = centre - below
                at_below, at_above = (1.0 - above).astype(jnp.bfloat16), above.astype(jnp.bfloat16)
                gap = (below.astype(jnp.int32) - depth).astype(jnp.int16)
                pieces = []
                for p in range(WINDOW // PIECE):
                    hit = jnp.where(gap == jnp.int16(p * PIECE - 1), at_above, zero)
                    pieces.append(jnp.where(gap == jnp.int16(p * PIECE), at_below, hit))
                weights = jnp.concatenate(pieces, axis=0)
                z0 = pl.multiple_of(block * 128, 128)
                tile = jnp.dot(
                    views[a, :, pl.ds(z0, WINDOW)], weights, preferred_element_type=jnp.float32
                )
                old = out[i, lane, cycle].astype(jnp.float32)
                out[i, lane, cycle] = (old + tile).astype(jnp.bfloat16)
        return carry

    most = functools.reduce(jnp.maximum, live)
    lax.fori_loop(0, lax.div(most + BATCH - 1, BATCH), some, 0)


def unit(hop, half, lanes, chips, here, sources, before=None):
    angles = HALF if half is not None else 2 * HALF
    narrow = sources[0][1].shape[1]
    smem = pl.BlockSpec(memory_space=pltpu.SMEM)
    vmem = pl.BlockSpec(memory_space=pltpu.VMEM)
    operands = [here] + [ref for source in sources for ref in source]
    specs = [smem] + [smem, vmem] * len(sources)
    if before is not None:
        operands, specs = operands + [before], specs + [vmem]
    return pl.pallas_call(
        functools.partial(unit_kernel, hop, half, lanes, chips),
        out_shape=jax.ShapeDtypeStruct((angles, lanes, TPO, narrow, TR), jnp.bfloat16),
        in_specs=specs,
        out_specs=vmem,
        scratch_shapes=[pltpu.SMEM((len(sources), angles * lanes + 1), jnp.int32)],
        compiler_params=pltpu.CompilerParams(vmem_limit_bytes=16 * 1024 * 1024),
        cost_estimate=pl.CostEstimate(
            flops=10**9 * len(sources), bytes_accessed=5 * 10**6 * len(sources), transcendentals=0
        ),
    )(*operands)


def add(*terms):
    total = terms[0].astype(jnp.float32)
    for term in terms[1:]:
        total = total + term.astype(jnp.float32)
    return total.astype(jnp.bfloat16)


def body(slab_views, footprint, row_shift, stretch, projections):
    n_grp = lax.axis_size("grp")
    n_ang = lax.axis_size("ang")
    chips = n_grp // 2
    owner = lax.axis_index("grp")
    chip, core = owner // 2, owner % 2
    views = slab_views[0]
    angles = views.shape[0]
    swap = [(i, i ^ 1) for i in range(n_grp)]
    onward = [(i, (i + (2 if i % 2 == 0 else -2)) % n_grp) for i in range(n_grp)]

    sibling_views = lax.ppermute(views, "grp", swap)
    lists = footprint[0]
    count = jnp.sum((lists >= 0).astype(jnp.int32), axis=-1)
    magnify = (TR * count).astype(jnp.float32) * stretch[0] / SZ
    meta = jnp.stack(
        [lists[:, 0].astype(jnp.float32), count.astype(jnp.float32), row_shift[0], 1.0 / magnify]
    )
    sibling_meta = lax.ppermute(meta, "grp", swap)
    here = jnp.stack([chip, core])
    near, far = (meta, views), (sibling_meta, sibling_views)

    early = unit(0, 0, 2, chips, here, [near])
    moving = [lax.ppermute(unit(0, 0, 2, chips, here, [far], early), "grp", onward), None]
    for hop in range(1, 4):
        for half in (1, 0):
            mine = unit(hop, half, 2, chips, here, [near, far])
            if moving[half] is not None:
                mine = add(moving[half], mine)
            moving[half] = lax.ppermute(mine, "grp", onward)
    kept = unit(4, None, 1, chips, here, [near, far])[:, 0]
    from_sibling = lax.ppermute(jnp.stack([moving[0][:, 1], moving[1][:, 1]]), "grp", swap)
    ready = (
        add(moving[0][:, 0], from_sibling[1], kept[:HALF]),
        add(moving[1][:, 0], from_sibling[0], kept[HALF:]),
    )
    summed = jnp.where(core == 0, jnp.concatenate(ready), jnp.concatenate(ready[::-1]))

    got = lax.all_to_all(summed, "ang", split_axis=0, concat_axis=0, tiled=True)
    columns = got.shape[0] * got.shape[2]
    rows = jnp.transpose(got, (1, 3, 0, 2)).reshape(TPO * TR, columns)
    basis = jnp.asarray(dft_basis(columns))
    n_freq = columns // 2
    spec_proj = jnp.dot(projections.reshape(-1, columns), basis, preferred_element_type=jnp.float32)
    spec_grad = jnp.dot(rows, basis, preferred_element_type=jnp.float32)
    product = (
        spec_grad[:, :n_freq] * spec_proj[:, :n_freq]
        + spec_grad[:, n_freq:] * spec_proj[:, n_freq:]
    )
    share = jnp.sum(product.reshape(TPO, TR, n_freq), axis=1).reshape(-1, 128)
    shares = lax.all_to_all(
        jnp.broadcast_to(share[None], (n_ang,) + share.shape), "ang", split_axis=0, concat_axis=0, tiled=True
    )
    filter_grad = (jnp.sum(shares, axis=0) * (1.0 / (columns * angles))).reshape(TPO, 1, n_freq)
    return rows.reshape(1, TPO, TR, columns), filter_grad


def solution(mesh):
    return jax.shard_map(
        body,
        mesh=mesh,
        in_specs=(
            P("grp", None, "ang", None),
            P("grp", None, None),
            P("grp", None),
            P("grp", None),
            P("ang", None, "grp", None),
        ),
        out_specs=(P("ang", None, "grp", None), P(None, "grp", None)),
        check_vma=False,
    )
```

```python
import functools
import math

import jax
import jax.numpy as jnp
import numpy as np
from jax import lax
from jax.experimental import pallas as pl
from jax.experimental.pallas import tpu as pltpu
from jax.sharding import PartitionSpec as P

TR = 128
KF = 8
SZ = 1024
TPO = 2
WINDOW = 512
HALF = 16
BATCH = 8
UNROLL = 16
PIECE = 16


def dft_basis(columns):
    column_idx = np.arange(columns, dtype=np.int64)[:, None]
    freq_idx = np.arange(columns // 2, dtype=np.int64)[None, :]
    phases = ((column_idx * freq_idx) % columns).astype(np.float64) * (2.0 * math.pi / columns)
    return np.concatenate([np.cos(phases), np.sin(phases)], axis=1).astype(jnp.bfloat16)


def unit_kernel(hop, lanes, chips, near, near_views, far, far_views, *refs):
    outs, (total, listed) = refs[:-2], refs[-2:]
    angles = total.shape[0]
    chip, core = near[4, 0].astype(jnp.int32), near[4, 1].astype(jnp.int32)
    reach = chips // 2 - hop
    target = lax.rem(chip + jnp.where(core == 0, reach, -reach) + chips, chips)
    owners = 2 * chips
    sources = ((near, near_views), (far, far_views))
    row = lax.broadcasted_iota(jnp.int32, (PIECE, TR), 1).astype(jnp.float32)
    depth = lax.broadcasted_iota(jnp.int32, (PIECE, TR), 0)
    zero = jnp.zeros((PIECE, TR), jnp.bfloat16)
    owner = [(2 * target + (core ^ lane)).astype(jnp.float32) for lane in range(lanes)]
    first_angle = core * HALF
    total[...] = jnp.zeros_like(total)

    def entry(meta, a, lane):
        k = owner[lane] - meta[0, a]
        k = jnp.where(k < 0.0, k + owners, k)
        return jnp.where(k < 0.0, k + owners, k)

    live = []
    for s, (meta, _) in enumerate(sources):

        def note(i, found):
            a = (first_angle + i) & (2 * HALF - 1)
            for lane in range(lanes):
                listed[s, found] = i * lanes + lane
                found = found + jnp.where(entry(meta, a, lane) < meta[1, a], 1, 0)
            return found

        live.append(lax.fori_loop(0, angles, note, jnp.int32(0), unroll=UNROLL))

    def some(at, carry):
        for m in range(BATCH):
            for s, (meta, views) in enumerate(sources):
                place = at * BATCH + m
                n = listed[s, jnp.clip(place, 0, jnp.maximum(live[s] - 1, 0))]
                i, lane = n >> (lanes - 1), n & (lanes - 1)
                a = (first_angle + i) & (2 * HALF - 1)
                k = entry(meta, a, 0) if lanes == 1 else jnp.where(
                    lane == 0, entry(meta, a, 0), entry(meta, a, 1)
                )
                slope = meta[3, a]
                begin = (TR * k - meta[2, a]) * slope
                block = jnp.clip((begin - 1.0).astype(jnp.int32) >> 7, 0, (SZ - WINDOW) // 128)
                start = jnp.where(place < live[s], begin - (128 * block).astype(jnp.float32), -1e4)
                cycle = jnp.where(meta[0, a] + k >= owners, 1, 0)
                centre = row * slope + start
                below = jnp.floor(centre)
                above = centre - below
                at_below = (1.0 - above).astype(jnp.bfloat16)
                at_above = above.astype(jnp.bfloat16)
                gap = (below.astype(jnp.int32) - depth).astype(jnp.int16)
                pieces = []
                for p in range(WINDOW // PIECE):
                    hit = jnp.where(gap == jnp.int16(p * PIECE - 1), at_above, zero)
                    pieces.append(jnp.where(gap == jnp.int16(p * PIECE), at_below, hit))
                weights = jnp.concatenate(pieces, axis=0)
                z0 = pl.multiple_of(block * 128, 128)
                total[i, lane, cycle] += jnp.dot(
                    views[a, :, pl.ds(z0, WINDOW)], weights, preferred_element_type=jnp.float32
                )
        return carry

    most = functools.reduce(jnp.maximum, live)
    lax.fori_loop(0, lax.div(most + BATCH - 1, BATCH), some, 0)
    for half, out in enumerate(outs):
        out[...] = total[half * HALF : (half + 1) * HALF].astype(jnp.bfloat16)


def units(hop, halves, lanes, chips, near, near_views, far, far_views):
    narrow = near_views.shape[1]
    smem = pl.BlockSpec(memory_space=pltpu.SMEM)
    vmem = pl.BlockSpec(memory_space=pltpu.VMEM)
    shape = (HALF, lanes, TPO, narrow, TR)
    return pl.pallas_call(
        functools.partial(unit_kernel, hop, lanes, chips),
        out_shape=[jax.ShapeDtypeStruct(shape, jnp.bfloat16)] * halves,
        in_specs=[smem, vmem, smem, vmem],
        out_specs=[vmem] * halves,
        scratch_shapes=[
            pltpu.VMEM((halves * HALF,) + shape[1:], jnp.float32),
            pltpu.SMEM((2, halves * HALF * lanes + 1), jnp.int32),
        ],
        compiler_params=pltpu.CompilerParams(vmem_limit_bytes=16 * 1024 * 1024),
        cost_estimate=pl.CostEstimate(
            flops=25 * 10**8 * halves, bytes_accessed=10**6, transcendentals=0
        ),
    )(near, near_views, far, far_views)


def add(*terms):
    total = terms[0].astype(jnp.float32)
    for term in terms[1:]:
        total = total + term.astype(jnp.float32)
    return total.astype(jnp.bfloat16)


def body(slab_views, footprint, row_shift, stretch, projections):
    n_grp = lax.axis_size("grp")
    n_ang = lax.axis_size("ang")
    chips = n_grp // 2
    owner = lax.axis_index("grp")
    chip, core = owner // 2, owner % 2
    views = slab_views[0]
    angles = views.shape[0]
    swap = [(i, i ^ 1) for i in range(n_grp)]
    onward = [(i, (i + (2 if i % 2 == 0 else -2)) % n_grp) for i in range(n_grp)]

    sibling_views = lax.ppermute(views, "grp", swap)
    lists = footprint[0]
    count = sum((lists[:, k] >= 0).astype(jnp.float32) for k in range(KF))
    magnify = TR * count * stretch[0] / SZ
    place = jnp.where(jnp.arange(angles) == 0, chip, core).astype(jnp.float32)
    meta = jnp.stack([lists[:, 0].astype(jnp.float32), count, row_shift[0], 1.0 / magnify, place])
    known = (chips, meta, views, lax.ppermute(meta, "grp", swap), sibling_views)

    moving = [lax.ppermute(units(0, 1, 2, *known)[0], "grp", onward), None]
    for hop in range(1, 4):
        mine = units(hop, 2, 2, *known)
        for half in (1, 0):
            sending = mine[half] if moving[half] is None else add(moving[half], mine[half])
            moving[half] = lax.ppermute(sending, "grp", onward)
    kept = [own[:, 0] for own in units(4, 2, 1, *known)]
    from_sibling = lax.ppermute(jnp.stack([moving[0][:, 1], moving[1][:, 1]]), "grp", swap)
    ready = (
        add(moving[0][:, 0], from_sibling[1], kept[0]),
        add(moving[1][:, 0], from_sibling[0], kept[1]),
    )
    summed = jnp.where(core == 0, jnp.concatenate(ready), jnp.concatenate(ready[::-1]))

    n_freq = n_ang * views.shape[1] // 2
    basis = jnp.asarray(dft_basis(2 * n_freq))
    spec_proj = jnp.dot(
        projections.reshape(-1, 2 * n_freq), basis, preferred_element_type=jnp.float32
    )
    summed, spec_proj = lax.optimization_barrier((summed, spec_proj))
    got = lax.all_to_all(summed, "ang", split_axis=0, concat_axis=0, tiled=True)
    rows = jnp.transpose(got, (1, 3, 0, 2)).reshape(TPO * TR, 2 * n_freq)
    spec_grad = jnp.dot(rows, basis, preferred_element_type=jnp.float32)
    product = (
        spec_grad[:, :n_freq] * spec_proj[:, :n_freq]
        + spec_grad[:, n_freq:] * spec_proj[:, n_freq:]
    )
    share = jnp.sum(product.reshape(TPO, TR, n_freq), axis=1).reshape(-1, 128)
    rows, share = lax.optimization_barrier((rows.reshape(1, TPO, TR, 2 * n_freq), share))
    shares = lax.all_to_all(
        jnp.broadcast_to(share[None], (n_ang,) + share.shape), "ang", split_axis=0, concat_axis=0, tiled=True
    )
    filter_grad = (jnp.sum(shares, axis=0) * (1.0 / (2 * n_freq * angles))).reshape(TPO, 1, n_freq)
    return rows, filter_grad


def solution(mesh):
    return jax.shard_map(
        body,
        mesh=mesh,
        in_specs=(
            P("grp", None, "ang", None),
            P("grp", None, None),
            P("grp", None),
            P("grp", None),
            P("ang", None, "grp", None),
        ),
        out_specs=(P("ang", None, "grp", None), P(None, "grp", None)),
        check_vma=False,
    )
```

```python
import functools
import math

import jax
import jax.numpy as jnp
import numpy as np
from jax import lax
from jax.experimental import pallas as pl
from jax.experimental.pallas import tpu as pltpu
from jax.sharding import PartitionSpec as P

TR = 128
KF = 8
SZ = 1024
TPO = 2
WINDOW = 512
HALF = 16
BATCH = 8
UNROLL = 16
PIECE = 16


def dft_basis(columns):
    column_idx = np.arange(columns, dtype=np.int64)[:, None]
    freq_idx = np.arange(columns // 2, dtype=np.int64)[None, :]
    phases = ((column_idx * freq_idx) % columns).astype(np.float64) * (2.0 * math.pi / columns)
    return np.concatenate([np.cos(phases), np.sin(phases)], axis=1).astype(jnp.bfloat16)


def unit_kernel(hop, lanes, chips, near, near_views, far, far_views, *refs):
    outs, (total, listed) = refs[:-2], refs[-2:]
    angles = total.shape[1]
    chip, core = near[4, 0].astype(jnp.int32), near[4, 1].astype(jnp.int32)
    reach = chips // 2 - hop
    target = lax.rem(chip + jnp.where(core == 0, reach, -reach) + chips, chips)
    owners = 2 * chips
    sources = ((near, near_views), (far, far_views))
    row = lax.broadcasted_iota(jnp.int32, (PIECE, TR), 1).astype(jnp.float32)
    depth = lax.broadcasted_iota(jnp.int32, (PIECE, TR), 0)
    zero = jnp.zeros((PIECE, TR), jnp.bfloat16)
    owner = [(2 * target + (core ^ lane)).astype(jnp.float32) for lane in range(lanes)]
    first_angle = core * HALF
    total[...] = jnp.zeros_like(total)

    def entry(meta, a, lane):
        k = owner[lane] - meta[0, a]
        k = jnp.where(k < 0.0, k + owners, k)
        return jnp.where(k < 0.0, k + owners, k)

    live = []
    for s, (meta, _) in enumerate(sources):

        def note(i, found):
            a = (first_angle + i) & (2 * HALF - 1)
            for lane in range(lanes):
                listed[s, found] = i * lanes + lane
                found = found + jnp.where(entry(meta, a, lane) < meta[1, a], 1, 0)
            return found

        live.append(lax.fori_loop(0, angles, note, jnp.int32(0), unroll=UNROLL))

    def some(at, carry):
        for m in range(BATCH):
            for s, (meta, views) in enumerate(sources):
                place = at * BATCH + m
                n = listed[s, jnp.clip(place, 0, jnp.maximum(live[s] - 1, 0))]
                i, lane = n >> (lanes - 1), n & (lanes - 1)
                a = (first_angle + i) & (2 * HALF - 1)
                k = entry(meta, a, 0) if lanes == 1 else jnp.where(
                    lane == 0, entry(meta, a, 0), entry(meta, a, 1)
                )
                slope = meta[3, a]
                begin = (TR * k - meta[2, a]) * slope
                block = jnp.clip((begin - 1.0).astype(jnp.int32) >> 7, 0, (SZ - WINDOW) // 128)
                start = jnp.where(place < live[s], begin - (128 * block).astype(jnp.float32), -1e4)
                cycle = jnp.where(meta[0, a] + k >= owners, 1, 0)
                centre = row * slope + start
                below = jnp.floor(centre)
                above = centre - below
                at_below = (1.0 - above).astype(jnp.bfloat16)
                at_above = above.astype(jnp.bfloat16)
                gap = (below.astype(jnp.int32) - depth).astype(jnp.int16)
                pieces = []
                for p in range(WINDOW // PIECE):
                    hit = jnp.where(gap == jnp.int16(p * PIECE - 1), at_above, zero)
                    pieces.append(jnp.where(gap == jnp.int16(p * PIECE), at_below, hit))
                weights = jnp.concatenate(pieces, axis=0)
                z0 = pl.multiple_of(block * 128, 128)
                total[lane, i, cycle] += jnp.dot(
                    views[a, :, pl.ds(z0, WINDOW)], weights, preferred_element_type=jnp.float32
                )
        return carry

    most = functools.reduce(jnp.maximum, live)
    lax.fori_loop(0, lax.div(most + BATCH - 1, BATCH), some, 0)
    for half, out in enumerate(outs):
        out[...] = total[:, half * HALF : (half + 1) * HALF].astype(jnp.bfloat16)


def units(hop, halves, lanes, chips, near, near_views, far, far_views):
    narrow = near_views.shape[1]
    smem = pl.BlockSpec(memory_space=pltpu.SMEM)
    vmem = pl.BlockSpec(memory_space=pltpu.VMEM)
    shape = (lanes, HALF, TPO, narrow, TR)
    return pl.pallas_call(
        functools.partial(unit_kernel, hop, lanes, chips),
        out_shape=[jax.ShapeDtypeStruct(shape, jnp.bfloat16)] * halves,
        in_specs=[smem, vmem, smem, vmem],
        out_specs=[vmem] * halves,
        scratch_shapes=[
            pltpu.VMEM((lanes, halves * HALF) + shape[2:], jnp.float32),
            pltpu.SMEM((2, halves * HALF * lanes + 1), jnp.int32),
        ],
        compiler_params=pltpu.CompilerParams(vmem_limit_bytes=16 * 1024 * 1024),
        cost_estimate=pl.CostEstimate(
            flops=25 * 10**8 * halves, bytes_accessed=10**6, transcendentals=0
        ),
    )(near, near_views, far, far_views)


def add(*terms):
    total = terms[0].astype(jnp.float32)
    for term in terms[1:]:
        total = total + term.astype(jnp.float32)
    return total.astype(jnp.bfloat16)


def finish_kernel(got, basis, spec_proj, rows, copies):
    n_freq = basis.shape[1] // 2
    blocks = n_freq // 128
    for p in range(TPO):
        turned = got[:, p].reshape(-1, TR).T
        rows[0, p] = turned
        spec_grad = jnp.dot(turned, basis[...], preferred_element_type=jnp.float32)
        both = spec_grad * spec_proj[p * TR : (p + 1) * TR]
        share = jnp.sum(both[:, :n_freq] + both[:, n_freq:], axis=0, keepdims=True)
        for n in range(blocks):
            block = jnp.broadcast_to(share[:, n * 128 : (n + 1) * 128], (copies.shape[0], 1, 128))
            copies[:, p * blocks + n : p * blocks + n + 1] = block


def finish(got, basis, spec_proj, n_ang):
    columns = basis.shape[0]
    vmem = pl.BlockSpec(memory_space=pltpu.VMEM)
    return pl.pallas_call(
        finish_kernel,
        out_shape=[
            jax.ShapeDtypeStruct((1, TPO, TR, columns), jnp.bfloat16),
            jax.ShapeDtypeStruct((n_ang, TPO * columns // 256, 128), jnp.float32),
        ],
        in_specs=[vmem] * 3,
        out_specs=[vmem] * 2,
        compiler_params=pltpu.CompilerParams(vmem_limit_bytes=24 * 1024 * 1024),
        cost_estimate=pl.CostEstimate(flops=10**9, bytes_accessed=10**6, transcendentals=0),
    )(got, basis, spec_proj)


def body(slab_views, footprint, row_shift, stretch, projections):
    n_grp = lax.axis_size("grp")
    n_ang = lax.axis_size("ang")
    chips = n_grp // 2
    owner = lax.axis_index("grp")
    chip, core = owner // 2, owner % 2
    views = slab_views[0]
    angles = views.shape[0]
    swap = [(i, i ^ 1) for i in range(n_grp)]
    onward = [(i, (i + (2 if i % 2 == 0 else -2)) % n_grp) for i in range(n_grp)]

    sibling_views = lax.ppermute(views, "grp", swap)
    lists = footprint[0]
    count = sum((lists[:, k] >= 0).astype(jnp.float32) for k in range(KF))
    magnify = TR * count * stretch[0] / SZ
    place = jnp.where(jnp.arange(angles) == 0, chip, core).astype(jnp.float32)
    meta = jnp.stack([lists[:, 0].astype(jnp.float32), count, row_shift[0], 1.0 / magnify, place])
    known = (chips, meta, views, lax.ppermute(meta, "grp", swap), sibling_views)

    across = [(i, j ^ 1) for i, j in onward]

    n_freq = n_ang * views.shape[1] // 2
    basis = jnp.asarray(dft_basis(2 * n_freq))
    spec_proj = jnp.dot(
        projections.reshape(-1, 2 * n_freq), basis, preferred_element_type=jnp.float32
    )

    first = lax.ppermute(units(0, 1, 2, *known)[0], "grp", onward)
    mine = units(1, 2, 2, *known)
    second = lax.ppermute(mine[1], "grp", onward)
    later = units(2, 2, 2, *known)
    sending, later, meta = lax.optimization_barrier((add(first, mine[0]), later, meta))
    first = lax.ppermute(sending, "grp", onward)
    known = known[:1] + (meta,) + known[2:]
    last = units(3, 2, 2, *known)
    sending, last = lax.optimization_barrier((add(second, later[1]), last))
    second = lax.ppermute(sending, "grp", onward)
    kept = units(4, 2, 1, *known)
    sending, kept = lax.optimization_barrier((add(first, later[0]), kept))
    first = lax.ppermute(sending, "grp", onward)
    sending, spec_proj = lax.optimization_barrier((add(second, last[1]), spec_proj))
    second = [lax.ppermute(sending[lane], "grp", (onward, across)[lane]) for lane in range(2)]
    sending = add(first, last[0])
    first = [lax.ppermute(sending[lane], "grp", (onward, across)[lane]) for lane in range(2)]
    ready = (
        add(first[0], second[1], kept[0][0]),
        add(second[0], first[1], kept[1][0]),
    )
    summed = jnp.where(core == 0, jnp.concatenate(ready), jnp.concatenate(ready[::-1]))

    got = lax.all_to_all(summed, "ang", split_axis=0, concat_axis=0, tiled=True)
    rows, copies = finish(got, basis, spec_proj, n_ang)
    shares = lax.all_to_all(copies, "ang", split_axis=0, concat_axis=0, tiled=True)
    filter_grad = (jnp.sum(shares, axis=0) * (1.0 / (2 * n_freq * angles))).reshape(TPO, 1, n_freq)
    return rows, filter_grad


def solution(mesh):
    return jax.shard_map(
        body,
        mesh=mesh,
        in_specs=(
            P("grp", None, "ang", None),
            P("grp", None, None),
            P("grp", None),
            P("grp", None),
            P("ang", None, "grp", None),
        ),
        out_specs=(P("ang", None, "grp", None), P(None, "grp", None)),
        check_vma=False,
    )
```

```python
import functools
import math

import jax
import jax.numpy as jnp
import numpy as np
from jax import lax
from jax.experimental import pallas as pl
from jax.experimental.pallas import tpu as pltpu
from jax.sharding import PartitionSpec as P

TR = 128
KF = 8
SZ = 1024
TPO = 2
WINDOW = 512
HALF = 16
BATCH = 8
UNROLL = 16
PIECE = 16


def dft_basis(columns):
    column_idx = np.arange(columns, dtype=np.int64)[:, None]
    freq_idx = np.arange(columns // 2, dtype=np.int64)[None, :]
    phases = ((column_idx * freq_idx) % columns).astype(np.float64) * (2.0 * math.pi / columns)
    return np.concatenate([np.cos(phases), np.sin(phases)], axis=1).astype(jnp.bfloat16)


def describe_kernel(lists, row_shift, stretch, place, meta):
    count = jnp.sum((lists[...] >= 0).astype(jnp.float32), axis=0, keepdims=True)
    lane = lax.broadcasted_iota(jnp.int32, count.shape, 1)
    meta[0:1] = lists[0:1].astype(jnp.float32)
    meta[1:2] = count
    meta[2:3] = row_shift[...]
    meta[3:4] = 1.0 / (TR * count * stretch[...] / SZ)
    meta[4:5] = jnp.where(lane == 0, place[0], place[1]).astype(jnp.float32)


def describe(lists, row_shift, stretch, place):
    vmem = pl.BlockSpec(memory_space=pltpu.VMEM)
    return pl.pallas_call(
        describe_kernel,
        out_shape=jax.ShapeDtypeStruct((5, lists.shape[1]), jnp.float32),
        in_specs=[vmem, vmem, vmem, pl.BlockSpec(memory_space=pltpu.SMEM)],
        out_specs=vmem,
    )(lists, row_shift, stretch, place)


def unit_kernel(hop, lanes, chips, near, near_views, far, far_views, *refs):
    outs, (total, listed) = refs[:-2], refs[-2:]
    angles = total.shape[1]
    chip, core = near[4, 0].astype(jnp.int32), near[4, 1].astype(jnp.int32)
    reach = chips // 2 - hop
    target = lax.rem(chip + jnp.where(core == 0, reach, -reach) + chips, chips)
    owners = 2 * chips
    sources = ((near, near_views), (far, far_views))
    row = lax.broadcasted_iota(jnp.int32, (PIECE, TR), 1).astype(jnp.float32)
    depth = lax.broadcasted_iota(jnp.int32, (PIECE, TR), 0)
    zero = jnp.zeros((PIECE, TR), jnp.bfloat16)
    owner = [(2 * target + (core ^ lane)).astype(jnp.float32) for lane in range(lanes)]
    first_angle = core * HALF
    total[...] = jnp.zeros_like(total)

    def entry(meta, a, lane):
        k = owner[lane] - meta[0, a]
        k = jnp.where(k < 0.0, k + owners, k)
        return jnp.where(k < 0.0, k + owners, k)

    live = []
    for s, (meta, _) in enumerate(sources):

        def note(i, found):
            a = (first_angle + i) & (2 * HALF - 1)
            for lane in range(lanes):
                listed[s, found] = i * lanes + lane
                found = found + jnp.where(entry(meta, a, lane) < meta[1, a], 1, 0)
            return found

        live.append(lax.fori_loop(0, angles, note, jnp.int32(0), unroll=UNROLL))

    def some(at, carry):
        for m in range(BATCH):
            for s, (meta, views) in enumerate(sources):
                place = at * BATCH + m
                n = listed[s, jnp.clip(place, 0, jnp.maximum(live[s] - 1, 0))]
                i, lane = n >> (lanes - 1), n & (lanes - 1)
                a = (first_angle + i) & (2 * HALF - 1)
                k = entry(meta, a, 0) if lanes == 1 else jnp.where(
                    lane == 0, entry(meta, a, 0), entry(meta, a, 1)
                )
                slope = meta[3, a]
                begin = (TR * k - meta[2, a]) * slope
                block = jnp.clip((begin - 1.0).astype(jnp.int32) >> 7, 0, (SZ - WINDOW) // 128)
                start = jnp.where(place < live[s], begin - (128 * block).astype(jnp.float32), -1e4)
                cycle = jnp.where(meta[0, a] + k >= owners, 1, 0)
                centre = row * slope + start
                below = jnp.floor(centre)
                above = centre - below
                at_below = (1.0 - above).astype(jnp.bfloat16)
                at_above = above.astype(jnp.bfloat16)
                gap = (below.astype(jnp.int32) - depth).astype(jnp.int16)
                pieces = []
                for p in range(WINDOW // PIECE):
                    hit = jnp.where(gap == jnp.int16(p * PIECE - 1), at_above, zero)
                    pieces.append(jnp.where(gap == jnp.int16(p * PIECE), at_below, hit))
                weights = jnp.concatenate(pieces, axis=0)
                z0 = pl.multiple_of(block * 128, 128)
                total[lane, i, cycle] += jnp.dot(
                    views[a, :, pl.ds(z0, WINDOW)], weights, preferred_element_type=jnp.float32
                )
        return carry

    most = functools.reduce(jnp.maximum, live)
    lax.fori_loop(0, lax.div(most + BATCH - 1, BATCH), some, 0)
    for half, out in enumerate(outs):
        out[...] = total[:, half * HALF : (half + 1) * HALF].astype(jnp.bfloat16)


def units(hop, halves, lanes, chips, near, near_views, far, far_views):
    narrow = near_views.shape[1]
    smem = pl.BlockSpec(memory_space=pltpu.SMEM)
    vmem = pl.BlockSpec(memory_space=pltpu.VMEM)
    shape = (lanes, HALF, TPO, narrow, TR)
    return pl.pallas_call(
        functools.partial(unit_kernel, hop, lanes, chips),
        out_shape=[jax.ShapeDtypeStruct(shape, jnp.bfloat16)] * halves,
        in_specs=[smem, vmem, smem, vmem],
        out_specs=[vmem] * halves,
        scratch_shapes=[
            pltpu.VMEM((lanes, halves * HALF) + shape[2:], jnp.float32),
            pltpu.SMEM((2, halves * HALF * lanes + 1), jnp.int32),
        ],
        compiler_params=pltpu.CompilerParams(vmem_limit_bytes=16 * 1024 * 1024),
        cost_estimate=pl.CostEstimate(
            flops=25 * 10**8 * halves, bytes_accessed=10**6, transcendentals=0
        ),
    )(near, near_views, far, far_views)


def add(*terms):
    total = terms[0].astype(jnp.float32)
    for term in terms[1:]:
        total = total + term.astype(jnp.float32)
    return total.astype(jnp.bfloat16)


def finish_kernel(got, basis, spec_proj, rows, copies):
    n_freq = basis.shape[1] // 2
    blocks = n_freq // 128
    for p in range(TPO):
        turned = got[:, p].reshape(-1, TR).T
        rows[0, p] = turned
        spec_grad = jnp.dot(turned, basis[...], preferred_element_type=jnp.float32)
        both = spec_grad * spec_proj[p * TR : (p + 1) * TR]
        share = jnp.sum(both[:, :n_freq] + both[:, n_freq:], axis=0, keepdims=True)
        for n in range(blocks):
            block = jnp.broadcast_to(share[:, n * 128 : (n + 1) * 128], (copies.shape[0], 1, 128))
            copies[:, p * blocks + n : p * blocks + n + 1] = block


def finish(got, basis, spec_proj, n_ang):
    columns = basis.shape[0]
    vmem = pl.BlockSpec(memory_space=pltpu.VMEM)
    return pl.pallas_call(
        finish_kernel,
        out_shape=[
            jax.ShapeDtypeStruct((1, TPO, TR, columns), jnp.bfloat16),
            jax.ShapeDtypeStruct((n_ang, TPO * columns // 256, 128), jnp.float32),
        ],
        in_specs=[vmem] * 3,
        out_specs=[vmem] * 2,
        compiler_params=pltpu.CompilerParams(vmem_limit_bytes=24 * 1024 * 1024),
        cost_estimate=pl.CostEstimate(flops=10**9, bytes_accessed=10**6, transcendentals=0),
    )(got, basis, spec_proj)


def body(slab_views, footprint, row_shift, stretch, projections):
    n_grp = lax.axis_size("grp")
    n_ang = lax.axis_size("ang")
    chips = n_grp // 2
    owner = lax.axis_index("grp")
    chip, core = owner // 2, owner % 2
    views = slab_views[0]
    angles = views.shape[0]
    swap = [(i, i ^ 1) for i in range(n_grp)]
    onward = [(i, (i + (2 if i % 2 == 0 else -2)) % n_grp) for i in range(n_grp)]

    sibling_views = lax.ppermute(views, "grp", swap)
    meta = describe(footprint[0].T, row_shift, stretch, jnp.stack([chip, core]))
    known = (chips, meta, views, lax.ppermute(meta, "grp", swap), sibling_views)

    n_freq = n_ang * views.shape[1] // 2
    basis = jnp.asarray(dft_basis(2 * n_freq))
    spec_proj = jnp.dot(
        projections.reshape(-1, 2 * n_freq), basis, preferred_element_type=jnp.float32
    )

    first = lax.ppermute(units(0, 1, 2, *known)[0], "grp", onward)
    mine = units(1, 2, 2, *known)
    second = lax.ppermute(mine[1], "grp", onward)
    kept = units(4, 2, 1, *known)
    sending, kept, meta = lax.optimization_barrier((add(first, mine[0]), kept, meta))
    known = known[:1] + (meta,) + known[2:]
    first = lax.ppermute(sending, "grp", onward)
    mine = units(2, 2, 2, *known)
    second = lax.ppermute(add(second, mine[1]), "grp", onward)
    first = lax.ppermute(add(first, mine[0]), "grp", onward)
    mine = units(3, 2, 2, *known)
    second = lax.ppermute(add(second, mine[1]), "grp", onward)
    first = lax.ppermute(add(first, mine[0]), "grp", onward)
    leaving, spec_proj = lax.optimization_barrier((jnp.stack([second[1], first[1]]), spec_proj))
    from_sibling = lax.ppermute(leaving, "grp", swap)
    ready = (
        add(first[0], from_sibling[0], kept[0][0]),
        add(second[0], from_sibling[1], kept[1][0]),
    )
    summed = jnp.where(core == 0, jnp.concatenate(ready), jnp.concatenate(ready[::-1]))

    got = lax.all_to_all(summed, "ang", split_axis=0, concat_axis=0, tiled=True)
    rows, copies = finish(got, basis, spec_proj, n_ang)
    shares = lax.all_to_all(copies, "ang", split_axis=0, concat_axis=0, tiled=True)
    filter_grad = (jnp.sum(shares, axis=0) * (1.0 / (2 * n_freq * angles))).reshape(TPO, 1, n_freq)
    return rows, filter_grad


def solution(mesh):
    return jax.shard_map(
        body,
        mesh=mesh,
        in_specs=(
            P("grp", None, "ang", None),
            P("grp", None, None),
            P("grp", None),
            P("grp", None),
            P("ang", None, "grp", None),
        ),
        out_specs=(P("ang", None, "grp", None), P(None, "grp", None)),
        check_vma=False,
    )
```

```python
import functools
import math

import jax
import jax.numpy as jnp
import numpy as np
from jax import lax
from jax.experimental import pallas as pl
from jax.experimental.pallas import tpu as pltpu
from jax.sharding import PartitionSpec as P

TR = 128
KF = 8
SZ = 1024
TPO = 2
WINDOW = 512
HALF = 16
BATCH = 8
UNROLL = 16
PIECE = 16


def dft_basis(columns):
    column_idx = np.arange(columns, dtype=np.int64)[:, None]
    freq_idx = np.arange(columns // 2, dtype=np.int64)[None, :]
    phases = ((column_idx * freq_idx) % columns).astype(np.float64) * (2.0 * math.pi / columns)
    return np.concatenate([np.cos(phases), np.sin(phases)], axis=1).astype(jnp.bfloat16)


def describe_kernel(lists, row_shift, stretch, meta):
    count = jnp.sum((lists[...] >= 0).astype(jnp.float32), axis=0, keepdims=True)
    meta[0:1] = lists[0:1].astype(jnp.float32)
    meta[1:2] = count
    meta[2:3] = row_shift[...]
    meta[3:4] = 1.0 / (TR * count * stretch[...] / SZ)


def describe(lists, row_shift, stretch):
    vmem = pl.BlockSpec(memory_space=pltpu.VMEM)
    return pl.pallas_call(
        describe_kernel,
        out_shape=jax.ShapeDtypeStruct((4, lists.shape[1]), jnp.float32),
        in_specs=[vmem] * 3,
        out_specs=vmem,
        compiler_params=pltpu.CompilerParams(vmem_limit_bytes=1024 * 1024),
    )(lists, row_shift, stretch)


def unit_kernel(hop, lanes, chips, slabs, resumed, fetched, place, *refs):
    sources = [refs[2 * s : 2 * s + 2] for s in range(slabs)]
    if fetched:
        refs, (brought, arrived) = refs[:-2], refs[-2:]
    outs, (total, listed) = refs[2 * slabs + resumed : -2], refs[-2:]
    angles = total.shape[1]
    chip, core = place[0], place[1]
    reach = chips // 2 - hop
    target = lax.rem(chip + jnp.where(core == 0, reach, -reach) + chips, chips)
    owners = 2 * chips
    row = lax.broadcasted_iota(jnp.int32, (PIECE, TR), 1).astype(jnp.float32)
    depth = lax.broadcasted_iota(jnp.int32, (PIECE, TR), 0)
    zero = jnp.zeros((PIECE, TR), jnp.bfloat16)
    owner = [(2 * target + (core ^ lane)).astype(jnp.float32) for lane in range(lanes)]
    first_angle = core * HALF
    if fetched:
        fetch = pltpu.make_async_copy(sources[0][1].at[pl.ds(first_angle, HALF)], brought, arrived)
        fetch.start()
    total[...] = refs[2 * slabs][...] if resumed else jnp.zeros_like(total)

    def entry(meta, a, lane):
        k = owner[lane] - meta[0, a]
        k = jnp.where(k < 0.0, k + owners, k)
        return jnp.where(k < 0.0, k + owners, k)

    live = []
    for s, (meta, _) in enumerate(sources):

        def note(i, found):
            a = (first_angle + i) & (2 * HALF - 1)
            for lane in range(lanes):
                listed[s, found] = i * lanes + lane
                found = found + jnp.where(entry(meta, a, lane) < meta[1, a], 1, 0)
            return found

        live.append(lax.fori_loop(0, angles, note, jnp.int32(0), unroll=UNROLL))

    if fetched:
        fetch.wait()

    def some(at, carry):
        for m in range(BATCH):
            for s, (meta, views) in enumerate(sources):
                place = at * BATCH + m
                n = listed[s, jnp.clip(place, 0, jnp.maximum(live[s] - 1, 0))]
                i, lane = n >> (lanes - 1), n & (lanes - 1)
                a = (first_angle + i) & (2 * HALF - 1)
                k = entry(meta, a, 0) if lanes == 1 else jnp.where(
                    lane == 0, entry(meta, a, 0), entry(meta, a, 1)
                )
                slope = meta[3, a]
                begin = (TR * k - meta[2, a]) * slope
                block = jnp.clip((begin - 1.0).astype(jnp.int32) >> 7, 0, (SZ - WINDOW) // 128)
                start = jnp.where(place < live[s], begin - (128 * block).astype(jnp.float32), -1e4)
                cycle = jnp.where(meta[0, a] + k >= owners, 1, 0)
                centre = row * slope + start
                below = jnp.floor(centre)
                above = centre - below
                at_below = (1.0 - above).astype(jnp.bfloat16)
                at_above = above.astype(jnp.bfloat16)
                gap = (below.astype(jnp.int32) - depth).astype(jnp.int16)
                pieces = []
                for p in range(WINDOW // PIECE):
                    hit = jnp.where(gap == jnp.int16(p * PIECE - 1), at_above, zero)
                    pieces.append(jnp.where(gap == jnp.int16(p * PIECE), at_below, hit))
                weights = jnp.concatenate(pieces, axis=0)
                z0 = pl.multiple_of(block * 128, 128)
                depths = pl.ds(z0, WINDOW)
                view = brought[i, :, depths] if fetched else views[a, :, depths]
                total[lane, i, cycle] += jnp.dot(view, weights, preferred_element_type=jnp.float32)
        return carry

    most = functools.reduce(jnp.maximum, live)
    lax.fori_loop(0, lax.div(most + BATCH - 1, BATCH), some, 0)
    for half, out in enumerate(outs):
        out[...] = total[:, half * HALF : (half + 1) * HALF].astype(out.dtype)


def units(hop, halves, lanes, chips, place, sources, before=None, fetched=False):
    narrow = sources[0][1].shape[1]
    smem = pl.BlockSpec(memory_space=pltpu.SMEM)
    vmem = pl.BlockSpec(memory_space=pltpu.VMEM)
    shape = (lanes, HALF, TPO, narrow, TR)
    operands = [place] + [ref for source in sources for ref in source]
    specs = [smem] + [smem, pl.BlockSpec(memory_space=pl.ANY) if fetched else vmem] * len(sources)
    scratch = [
        pltpu.VMEM((lanes, halves * HALF) + shape[2:], jnp.float32),
        pltpu.SMEM((len(sources), halves * HALF * lanes + 1), jnp.int32),
    ]
    if fetched:
        scratch += [pltpu.VMEM((HALF,) + sources[0][1].shape[1:], jnp.bfloat16), pltpu.SemaphoreType.DMA]
    dtype = jnp.float32 if fetched else jnp.bfloat16
    if before is not None:
        operands, specs = operands + [before], specs + [vmem]
    return pl.pallas_call(
        functools.partial(
            unit_kernel, hop, lanes, chips, len(sources), before is not None, fetched
        ),
        out_shape=[jax.ShapeDtypeStruct(shape, dtype)] * halves,
        in_specs=specs,
        out_specs=[vmem] * halves,
        scratch_shapes=scratch,
        compiler_params=pltpu.CompilerParams(vmem_limit_bytes=12 * 1024 * 1024),
        cost_estimate=pl.CostEstimate(
            flops=12 * 10**8 * halves * len(sources), bytes_accessed=10**6, transcendentals=0
        ),
    )(*operands)


def close_kernel(place, here, there, mine, other_here, other_there, other_mine, out):
    core = place[1]
    for half, terms in enumerate(((here, there, mine), (other_here, other_there, other_mine))):
        total = sum(term[...].astype(jnp.float32) for term in terms)
        out[pl.ds((core ^ half) * HALF, HALF)] = total.astype(jnp.bfloat16)


def close(place, *terms):
    smem = pl.BlockSpec(memory_space=pltpu.SMEM)
    vmem = pl.BlockSpec(memory_space=pltpu.VMEM)
    return pl.pallas_call(
        close_kernel,
        out_shape=jax.ShapeDtypeStruct((2 * HALF,) + terms[0].shape[1:], jnp.bfloat16),
        in_specs=[smem] + [vmem] * len(terms),
        out_specs=vmem,
        compiler_params=pltpu.CompilerParams(vmem_limit_bytes=6 * 1024 * 1024),
    )(place, *terms)


def add(*terms):
    total = terms[0].astype(jnp.float32)
    for term in terms[1:]:
        total = total + term.astype(jnp.float32)
    return total.astype(jnp.bfloat16)


def finish_kernel(got, basis, spec_proj, rows, copies):
    n_freq = basis.shape[1] // 2
    blocks = n_freq // 128
    for p in range(TPO):
        turned = got[:, p].reshape(-1, TR).T
        rows[0, p] = turned
        spec_grad = jnp.dot(turned, basis[...], preferred_element_type=jnp.float32)
        both = spec_grad * spec_proj[p * TR : (p + 1) * TR]
        share = jnp.sum(both[:, :n_freq] + both[:, n_freq:], axis=0, keepdims=True)
        for n in range(blocks):
            block = jnp.broadcast_to(share[:, n * 128 : (n + 1) * 128], (copies.shape[0], 1, 128))
            copies[:, p * blocks + n : p * blocks + n + 1] = block


def finish(got, basis, spec_proj, n_ang):
    columns = basis.shape[0]
    vmem = pl.BlockSpec(memory_space=pltpu.VMEM)
    return pl.pallas_call(
        finish_kernel,
        out_shape=[
            jax.ShapeDtypeStruct((1, TPO, TR, columns), jnp.bfloat16),
            jax.ShapeDtypeStruct((n_ang, TPO * columns // 256, 128), jnp.float32),
        ],
        in_specs=[vmem] * 3,
        out_specs=[vmem] * 2,
        compiler_params=pltpu.CompilerParams(vmem_limit_bytes=12 * 1024 * 1024),
        cost_estimate=pl.CostEstimate(flops=10**9, bytes_accessed=10**6, transcendentals=0),
    )(got, basis, spec_proj)


def body(slab_views, footprint, row_shift, stretch, projections):
    n_grp = lax.axis_size("grp")
    n_ang = lax.axis_size("ang")
    chips = n_grp // 2
    owner = lax.axis_index("grp")
    chip, core = owner // 2, owner % 2
    views = slab_views[0]
    angles = views.shape[0]
    swap = [(i, i ^ 1) for i in range(n_grp)]
    onward = [(i, (i + (2 if i % 2 == 0 else -2)) % n_grp) for i in range(n_grp)]

    sibling_views = lax.ppermute(views, "grp", swap)
    place = jnp.stack([chip, core])
    meta = describe(footprint[0].T, row_shift, stretch)
    near, far = (meta, views), (lax.ppermute(meta, "grp", swap), sibling_views)
    known = (2, chips, place, [near, far])

    n_freq = n_ang * views.shape[1] // 2
    basis = jnp.asarray(dft_basis(2 * n_freq))
    spec_proj = jnp.dot(
        projections.reshape(-1, 2 * n_freq), basis, preferred_element_type=jnp.float32
    )

    early = units(0, 1, 2, chips, place, [near], fetched=True)[0]
    first = lax.ppermute(units(0, 1, 2, chips, place, [far], early)[0], "grp", onward)
    mine = units(1, 2, *known)
    second = lax.ppermute(mine[1], "grp", onward)
    kept = units(4, 2, 1, *known[1:])
    sending, kept, place = lax.optimization_barrier((add(first, mine[0]), kept, place))
    known = (2, chips, place, [near, far])
    first = lax.ppermute(sending, "grp", onward)
    mine = units(2, 2, *known)
    second = lax.ppermute(add(second, mine[1]), "grp", onward)
    first = lax.ppermute(add(first, mine[0]), "grp", onward)
    mine = units(3, 2, *known)
    second = lax.ppermute(add(second, mine[1]), "grp", onward)
    first = lax.ppermute(add(first, mine[0]), "grp", onward)
    to_first = lax.ppermute(second[1], "grp", swap)
    leaving, spec_proj = lax.optimization_barrier((first[1], spec_proj))
    to_second = lax.ppermute(leaving, "grp", swap)
    summed = close(place, first[0], to_first, kept[0][0], second[0], to_second, kept[1][0])

    got = lax.all_to_all(summed, "ang", split_axis=0, concat_axis=0, tiled=True)
    rows, copies = finish(got, basis, spec_proj, n_ang)
    shares = lax.all_to_all(copies, "ang", split_axis=0, concat_axis=0, tiled=True)
    filter_grad = (jnp.sum(shares, axis=0) * (1.0 / (2 * n_freq * angles))).reshape(TPO, 1, n_freq)
    return rows, filter_grad


def solution(mesh):
    return jax.shard_map(
        body,
        mesh=mesh,
        in_specs=(
            P("grp", None, "ang", None),
            P("grp", None, None),
            P("grp", None),
            P("grp", None),
            P("ang", None, "grp", None),
        ),
        out_specs=(P("ang", None, "grp", None), P(None, "grp", None)),
        check_vma=False,
    )
```

```python
import functools
import math

import jax
import jax.numpy as jnp
import numpy as np
from jax import lax
from jax.experimental import pallas as pl
from jax.experimental.pallas import tpu as pltpu
from jax.sharding import PartitionSpec as P

TR = 128
KF = 8
SZ = 1024
TPO = 2
WINDOW = 512
HALF = 16
BATCH = 8
UNROLL = 16
PIECE = 16


def dft_basis(columns):
    column_idx = np.arange(columns, dtype=np.int64)[:, None]
    freq_idx = np.arange(columns // 2, dtype=np.int64)[None, :]
    phases = ((column_idx * freq_idx) % columns).astype(np.float64) * (2.0 * math.pi / columns)
    return np.concatenate([np.cos(phases), np.sin(phases)], axis=1).astype(jnp.bfloat16)


def describe_kernel(lists, row_shift, stretch, meta, *held):
    held, arrived = held[:-1], held[-1]
    fetches = [
        pltpu.make_async_copy(source, target, arrived.at[n])
        for n, (source, target) in enumerate(zip((lists, row_shift, stretch), held))
    ]
    for fetch in fetches:
        fetch.start()
    for fetch in fetches:
        fetch.wait()
    count = jnp.sum((held[0][...] >= 0).astype(jnp.float32), axis=0, keepdims=True)
    meta[0:1] = held[0][0:1].astype(jnp.float32)
    meta[1:2] = count
    meta[2:3] = held[1][...]
    meta[3:4] = 1.0 / (TR * count * held[2][...] / SZ)


def describe(*operands):
    return pl.pallas_call(
        describe_kernel,
        out_shape=jax.ShapeDtypeStruct((4, operands[0].shape[1]), jnp.float32),
        in_specs=[pl.BlockSpec(memory_space=pltpu.HBM)] * 3,
        out_specs=pl.BlockSpec(memory_space=pltpu.VMEM),
        scratch_shapes=[pltpu.VMEM(operand.shape, operand.dtype) for operand in operands]
        + [pltpu.SemaphoreType.DMA((3,))],
        compiler_params=pltpu.CompilerParams(vmem_limit_bytes=1024 * 1024),
    )(*(pltpu.with_memory_space_constraint(operand, pltpu.HBM) for operand in operands))


def unit_kernel(hop, lanes, chips, slabs, resumed, fetched, place, *refs):
    sources = [refs[2 * s : 2 * s + 2] for s in range(slabs)]
    if fetched:
        refs, (brought, arrived) = refs[:-2], refs[-2:]
    outs, (total, listed) = refs[2 * slabs + resumed : -2], refs[-2:]
    angles = total.shape[1]
    chip, core = place[0], place[1]
    reach = chips // 2 - hop
    target = lax.rem(chip + jnp.where(core == 0, reach, -reach) + chips, chips)
    owners = 2 * chips
    row = lax.broadcasted_iota(jnp.int32, (PIECE, TR), 1).astype(jnp.float32)
    depth = lax.broadcasted_iota(jnp.int32, (PIECE, TR), 0)
    zero = jnp.zeros((PIECE, TR), jnp.bfloat16)
    owner = [(2 * target + (core ^ lane)).astype(jnp.float32) for lane in range(lanes)]
    first_angle = core * HALF
    if fetched:
        fetch = pltpu.make_async_copy(sources[0][1].at[pl.ds(first_angle, HALF)], brought, arrived)
        fetch.start()
    total[...] = refs[2 * slabs][...] if resumed else jnp.zeros_like(total)

    def entry(meta, a, lane):
        k = owner[lane] - meta[0, a]
        k = jnp.where(k < 0.0, k + owners, k)
        return jnp.where(k < 0.0, k + owners, k)

    live = []
    for s, (meta, _) in enumerate(sources):

        def note(i, found):
            a = (first_angle + i) & (2 * HALF - 1)
            for lane in range(lanes):
                listed[s, found] = i * lanes + lane
                found = found + jnp.where(entry(meta, a, lane) < meta[1, a], 1, 0)
            return found

        live.append(lax.fori_loop(0, angles, note, jnp.int32(0), unroll=UNROLL))

    if fetched:
        fetch.wait()

    def some(at, carry):
        for m in range(BATCH):
            for s, (meta, views) in enumerate(sources):
                place = at * BATCH + m
                n = listed[s, jnp.clip(place, 0, jnp.maximum(live[s] - 1, 0))]
                i, lane = n >> (lanes - 1), n & (lanes - 1)
                a = (first_angle + i) & (2 * HALF - 1)
                k = entry(meta, a, 0) if lanes == 1 else jnp.where(
                    lane == 0, entry(meta, a, 0), entry(meta, a, 1)
                )
                slope = meta[3, a]
                begin = (TR * k - meta[2, a]) * slope
                block = jnp.clip((begin - 1.0).astype(jnp.int32) >> 7, 0, (SZ - WINDOW) // 128)
                start = jnp.where(place < live[s], begin - (128 * block).astype(jnp.float32), -1e4)
                cycle = jnp.where(meta[0, a] + k >= owners, 1, 0)
                centre = row * slope + start
                below = jnp.floor(centre)
                above = centre - below
                at_below = (1.0 - above).astype(jnp.bfloat16)
                at_above = above.astype(jnp.bfloat16)
                gap = (below.astype(jnp.int32) - depth).astype(jnp.int16)
                pieces = []
                for p in range(WINDOW // PIECE):
                    hit = jnp.where(gap == jnp.int16(p * PIECE - 1), at_above, zero)
                    pieces.append(jnp.where(gap == jnp.int16(p * PIECE), at_below, hit))
                weights = jnp.concatenate(pieces, axis=0)
                z0 = pl.multiple_of(block * 128, 128)
                depths = pl.ds(z0, WINDOW)
                view = brought[i, :, depths] if fetched else views[a, :, depths]
                total[lane, i, cycle] += jnp.dot(view, weights, preferred_element_type=jnp.float32)
        return carry

    most = functools.reduce(jnp.maximum, live)
    lax.fori_loop(0, lax.div(most + BATCH - 1, BATCH), some, 0)
    for half, out in enumerate(outs):
        out[...] = total[:, half * HALF : (half + 1) * HALF].astype(out.dtype)


def units(hop, halves, lanes, chips, place, sources, before=None, fetched=False):
    narrow = sources[0][1].shape[1]
    smem = pl.BlockSpec(memory_space=pltpu.SMEM)
    vmem = pl.BlockSpec(memory_space=pltpu.VMEM)
    shape = (lanes, HALF, TPO, narrow, TR)
    operands = [place] + [ref for source in sources for ref in source]
    specs = [smem] + [smem, pl.BlockSpec(memory_space=pltpu.HBM) if fetched else vmem] * len(sources)
    scratch = [
        pltpu.VMEM((lanes, halves * HALF) + shape[2:], jnp.float32),
        pltpu.SMEM((len(sources), halves * HALF * lanes + 1), jnp.int32),
    ]
    if fetched:
        operands[2] = pltpu.with_memory_space_constraint(operands[2], pltpu.HBM)
        scratch += [pltpu.VMEM((HALF,) + sources[0][1].shape[1:], jnp.bfloat16), pltpu.SemaphoreType.DMA]
    dtype = jnp.float32 if fetched else jnp.bfloat16
    if before is not None:
        operands, specs = operands + [before], specs + [vmem]
    return pl.pallas_call(
        functools.partial(
            unit_kernel, hop, lanes, chips, len(sources), before is not None, fetched
        ),
        out_shape=[jax.ShapeDtypeStruct(shape, dtype)] * halves,
        in_specs=specs,
        out_specs=[vmem] * halves,
        scratch_shapes=scratch,
        compiler_params=pltpu.CompilerParams(vmem_limit_bytes=12 * 1024 * 1024),
        cost_estimate=pl.CostEstimate(
            flops=12 * 10**8 * halves * len(sources), bytes_accessed=10**6, transcendentals=0
        ),
    )(*operands)


def close_kernel(place, here, there, mine, other_here, other_there, other_mine, out):
    core = place[1]
    for half, terms in enumerate(((here, there, mine), (other_here, other_there, other_mine))):
        total = sum(term[...].astype(jnp.float32) for term in terms)
        out[pl.ds((core ^ half) * HALF, HALF)] = total.astype(jnp.bfloat16)


def close(place, *terms):
    smem = pl.BlockSpec(memory_space=pltpu.SMEM)
    vmem = pl.BlockSpec(memory_space=pltpu.VMEM)
    return pl.pallas_call(
        close_kernel,
        out_shape=jax.ShapeDtypeStruct((2 * HALF,) + terms[0].shape[1:], jnp.bfloat16),
        in_specs=[smem] + [vmem] * len(terms),
        out_specs=vmem,
        compiler_params=pltpu.CompilerParams(vmem_limit_bytes=6 * 1024 * 1024),
    )(place, *terms)


def add(*terms):
    total = terms[0].astype(jnp.float32)
    for term in terms[1:]:
        total = total + term.astype(jnp.float32)
    return total.astype(jnp.bfloat16)


def finish_kernel(got, basis, spec_proj, rows, copies):
    n_freq = basis.shape[1] // 2
    blocks = n_freq // 128
    for p in range(TPO):
        turned = got[:, p].reshape(-1, TR).T
        rows[0, p] = turned
        spec_grad = jnp.dot(turned, basis[...], preferred_element_type=jnp.float32)
        both = spec_grad * spec_proj[p * TR : (p + 1) * TR]
        share = jnp.sum(both[:, :n_freq] + both[:, n_freq:], axis=0, keepdims=True)
        for n in range(blocks):
            block = jnp.broadcast_to(share[:, n * 128 : (n + 1) * 128], (copies.shape[0], 1, 128))
            copies[:, p * blocks + n : p * blocks + n + 1] = block


def finish(got, basis, spec_proj, n_ang):
    columns = basis.shape[0]
    vmem = pl.BlockSpec(memory_space=pltpu.VMEM)
    return pl.pallas_call(
        finish_kernel,
        out_shape=[
            jax.ShapeDtypeStruct((1, TPO, TR, columns), jnp.bfloat16),
            jax.ShapeDtypeStruct((n_ang, TPO * columns // 256, 128), jnp.float32),
        ],
        in_specs=[vmem] * 3,
        out_specs=[vmem] * 2,
        compiler_params=pltpu.CompilerParams(vmem_limit_bytes=12 * 1024 * 1024),
        cost_estimate=pl.CostEstimate(flops=10**9, bytes_accessed=10**6, transcendentals=0),
    )(got, basis, spec_proj)


def body(slab_views, footprint, row_shift, stretch, projections):
    n_grp = lax.axis_size("grp")
    n_ang = lax.axis_size("ang")
    chips = n_grp // 2
    owner = lax.axis_index("grp")
    chip, core = owner // 2, owner % 2
    views = slab_views[0]
    angles = views.shape[0]
    swap = [(i, i ^ 1) for i in range(n_grp)]
    onward = [(i, (i + (2 if i % 2 == 0 else -2)) % n_grp) for i in range(n_grp)]

    sibling_views = lax.ppermute(views, "grp", swap)
    place = jnp.stack([chip, core])
    meta = describe(footprint[0].T, row_shift, stretch)
    near, far = (meta, views), (lax.ppermute(meta, "grp", swap), sibling_views)
    known = (2, chips, place, [near, far])

    n_freq = n_ang * views.shape[1] // 2
    basis = jnp.asarray(dft_basis(2 * n_freq))
    spec_proj = jnp.dot(
        projections.reshape(-1, 2 * n_freq), basis, preferred_element_type=jnp.float32
    )

    early = units(0, 1, 2, chips, place, [near], fetched=True)[0]
    first = lax.ppermute(units(0, 1, 2, chips, place, [far], early)[0], "grp", onward)
    mine = units(1, 2, *known)
    second = lax.ppermute(mine[1], "grp", onward)
    kept = units(4, 2, 1, *known[1:])
    sending, kept, place = lax.optimization_barrier((add(first, mine[0]), kept, place))
    known = (2, chips, place, [near, far])
    first = lax.ppermute(sending, "grp", onward)
    mine = units(2, 2, *known)
    second = lax.ppermute(add(second, mine[1]), "grp", onward)
    first = lax.ppermute(add(first, mine[0]), "grp", onward)
    mine = units(3, 2, *known)
    second = lax.ppermute(add(second, mine[1]), "grp", onward)
    first = lax.ppermute(add(first, mine[0]), "grp", onward)
    to_first = lax.ppermute(second[1], "grp", swap)
    leaving, spec_proj = lax.optimization_barrier((first[1], spec_proj))
    to_second = lax.ppermute(leaving, "grp", swap)
    summed = close(place, first[0], to_first, kept[0][0], second[0], to_second, kept[1][0])

    got = lax.all_to_all(summed, "ang", split_axis=0, concat_axis=0, tiled=True)
    rows, copies = finish(got, basis, spec_proj, n_ang)
    shares = lax.all_to_all(copies, "ang", split_axis=0, concat_axis=0, tiled=True)
    filter_grad = (jnp.sum(shares, axis=0) * (1.0 / (2 * n_freq * angles))).reshape(TPO, 1, n_freq)
    return rows, filter_grad


def solution(mesh):
    return jax.shard_map(
        body,
        mesh=mesh,
        in_specs=(
            P("grp", None, "ang", None),
            P("grp", None, None),
            P("grp", None),
            P("grp", None),
            P("ang", None, "grp", None),
        ),
        out_specs=(P("ang", None, "grp", None), P(None, "grp", None)),
        check_vma=False,
    )
```

```python
import functools
import math

import jax
import jax.numpy as jnp
import numpy as np
from jax import lax
from jax.experimental import pallas as pl
from jax.experimental.pallas import tpu as pltpu
from jax.sharding import PartitionSpec as P

TR = 128
KF = 8
SZ = 1024
TPO = 2
WINDOW = 512
HALF = 16
BATCH = 8
FEW = KF // 2
UNROLL = 16
PIECE = 16


def dft_basis(columns):
    column_idx = np.arange(columns, dtype=np.int64)[:, None]
    freq_idx = np.arange(columns // 2, dtype=np.int64)[None, :]
    phases = ((column_idx * freq_idx) % columns).astype(np.float64) * (2.0 * math.pi / columns)
    return np.concatenate([np.cos(phases), np.sin(phases)], axis=1).astype(jnp.bfloat16)


def describe_kernel(lists, row_shift, stretch, meta, *held):
    held, arrived = held[:-1], held[-1]
    fetches = [
        pltpu.make_async_copy(source, target, arrived.at[n])
        for n, (source, target) in enumerate(zip((lists, row_shift, stretch), held))
    ]
    for fetch in fetches:
        fetch.start()
    for fetch in fetches:
        fetch.wait()
    count = jnp.sum((held[0][...] >= 0).astype(jnp.float32), axis=0, keepdims=True)
    meta[0:1] = held[0][0:1].astype(jnp.float32)
    meta[1:2] = count
    meta[2:3] = held[1][...]
    meta[3:4] = 1.0 / (TR * count * held[2][...] / SZ)


def describe(*operands):
    return pl.pallas_call(
        describe_kernel,
        out_shape=jax.ShapeDtypeStruct((4, operands[0].shape[1]), jnp.float32),
        in_specs=[pl.BlockSpec(memory_space=pltpu.HBM)] * 3,
        out_specs=pl.BlockSpec(memory_space=pltpu.VMEM),
        scratch_shapes=[pltpu.VMEM(operand.shape, operand.dtype) for operand in operands]
        + [pltpu.SemaphoreType.DMA((3,))],
        compiler_params=pltpu.CompilerParams(vmem_limit_bytes=1024 * 1024),
    )(*(pltpu.with_memory_space_constraint(operand, pltpu.HBM) for operand in operands))


def unit_kernel(hop, lanes, chips, slabs, resumed, fetched, place, *refs):
    sources = [refs[2 * s : 2 * s + 2] for s in range(slabs)]
    if fetched:
        refs, (brought, arrived) = refs[:-2], refs[-2:]
    outs, (total, listed) = refs[2 * slabs + resumed : -2], refs[-2:]
    angles = total.shape[1]
    chip, core = place[0], place[1]
    reach = chips // 2 - hop
    target = lax.rem(chip + jnp.where(core == 0, reach, -reach) + chips, chips)
    owners = 2 * chips
    row = lax.broadcasted_iota(jnp.int32, (PIECE, TR), 1).astype(jnp.float32)
    depth = lax.broadcasted_iota(jnp.int32, (PIECE, TR), 0)
    zero = jnp.zeros((PIECE, TR), jnp.bfloat16)
    owner = [(2 * target + (core ^ lane)).astype(jnp.float32) for lane in range(lanes)]
    first_angle = core * HALF
    size = angles * lanes + 1
    if fetched:
        fetch = pltpu.make_async_copy(sources[0][1].at[pl.ds(first_angle, HALF)], brought, arrived)
        fetch.start()
    total[...] = refs[2 * slabs][...] if resumed else jnp.zeros_like(total)

    def entry(meta, a, wanted):
        k = wanted - meta[0, a]
        k = jnp.where(k < 0.0, k + owners, k)
        return jnp.where(k < 0.0, k + owners, k)

    ends = []
    for s, (meta, _) in enumerate(sources):

        def note(i, found):
            a = (first_angle + i) & (2 * HALF - 1)
            count = meta[1, a]
            few = count < FEW + 1
            wide, narrow = found
            for lane in range(lanes):
                live = entry(meta, a, owner[lane]) < count
                listed[s, jnp.where(few, size - wide, narrow)] = i * lanes + lane
                wide = wide + jnp.where(live & few, 1, 0)
                narrow = narrow + jnp.where(live & ~few, 1, 0)
            return wide, narrow

        ends.append(
            lax.fori_loop(0, angles, note, (jnp.int32(0), jnp.int32(0)), unroll=UNROLL)
        )

    if fetched:
        fetch.wait()

    def add_tiles(window, batch, live, at_place):
        limits = [jnp.maximum(n - 1, 0) for n in live]

        def some(at, carry):
            for m in range(batch):
                for s, (meta, views) in enumerate(sources):
                    place = at * batch + m
                    n = listed[s, at_place(jnp.minimum(place, limits[s]))]
                    i, lane = n >> (lanes - 1), n & (lanes - 1)
                    a = (first_angle + i) & (2 * HALF - 1)
                    wanted = owner[0] if lanes == 1 else jnp.where(lane == 0, owner[0], owner[1])
                    k = entry(meta, a, wanted)
                    begin = (TR * k - meta[2, a]) * meta[3, a]
                    block = jnp.clip((begin - 1.0).astype(jnp.int32) >> 7, 0, (SZ - window) // 128)
                    start = jnp.where(
                        place < live[s], begin - (128 * block).astype(jnp.float32), -1e4
                    )
                    cycle = jnp.where(meta[0, a] + k >= owners, 1, 0)
                    centre = row * meta[3, a] + start
                    below = jnp.floor(centre)
                    above = centre - below
                    at_below = (1.0 - above).astype(jnp.bfloat16)
                    at_above = above.astype(jnp.bfloat16)
                    gap = (below.astype(jnp.int32) - depth).astype(jnp.int16)
                    pieces = []
                    for p in range(window // PIECE):
                        hit = jnp.where(gap == jnp.int16(p * PIECE - 1), at_above, zero)
                        pieces.append(jnp.where(gap == jnp.int16(p * PIECE), at_below, hit))
                    weights = jnp.concatenate(pieces, axis=0)
                    depths = pl.ds(pl.multiple_of(block * 128, 128), window)
                    view = brought[i, :, depths] if fetched else views[a, :, depths]
                    total[lane, i, cycle] += jnp.dot(
                        view, weights, preferred_element_type=jnp.float32
                    )
            return carry

        most = functools.reduce(jnp.maximum, live)
        lax.fori_loop(0, lax.div(most + batch - 1, batch), some, 0)

    add_tiles(WINDOW, BATCH // 4, [wide for wide, _ in ends], lambda n: size - n)
    add_tiles(WINDOW - 128, BATCH, [narrow for _, narrow in ends], lambda n: n)
    for half, out in enumerate(outs):
        out[...] = total[:, half * HALF : (half + 1) * HALF].astype(out.dtype)


def units(hop, halves, lanes, chips, place, sources, before=None, fetched=False):
    narrow = sources[0][1].shape[1]
    smem = pl.BlockSpec(memory_space=pltpu.SMEM)
    vmem = pl.BlockSpec(memory_space=pltpu.VMEM)
    shape = (lanes, HALF, TPO, narrow, TR)
    operands = [place] + [ref for source in sources for ref in source]
    specs = [smem] + [smem, pl.BlockSpec(memory_space=pltpu.HBM) if fetched else vmem] * len(sources)
    scratch = [
        pltpu.VMEM((lanes, halves * HALF) + shape[2:], jnp.float32),
        pltpu.SMEM((len(sources), halves * HALF * lanes + 2), jnp.int32),
    ]
    if fetched:
        operands[2] = pltpu.with_memory_space_constraint(operands[2], pltpu.HBM)
        scratch += [pltpu.VMEM((HALF,) + sources[0][1].shape[1:], jnp.bfloat16), pltpu.SemaphoreType.DMA]
    dtype = jnp.float32 if fetched else jnp.bfloat16
    if before is not None:
        operands, specs = operands + [before], specs + [vmem]
    return pl.pallas_call(
        functools.partial(
            unit_kernel, hop, lanes, chips, len(sources), before is not None, fetched
        ),
        out_shape=[jax.ShapeDtypeStruct(shape, dtype)] * halves,
        in_specs=specs,
        out_specs=[vmem] * halves,
        scratch_shapes=scratch,
        compiler_params=pltpu.CompilerParams(vmem_limit_bytes=12 * 1024 * 1024),
        cost_estimate=pl.CostEstimate(
            flops=12 * 10**8 * halves * len(sources), bytes_accessed=10**6, transcendentals=0
        ),
    )(*operands)


def close_kernel(place, here, there, mine, other_here, other_there, other_mine, out):
    core = place[1]
    for half, terms in enumerate(((here, there, mine), (other_here, other_there, other_mine))):
        total = sum(term[...].astype(jnp.float32) for term in terms)
        out[pl.ds((core ^ half) * HALF, HALF)] = total.astype(jnp.bfloat16)


def close(place, *terms):
    smem = pl.BlockSpec(memory_space=pltpu.SMEM)
    vmem = pl.BlockSpec(memory_space=pltpu.VMEM)
    return pl.pallas_call(
        close_kernel,
        out_shape=jax.ShapeDtypeStruct((2 * HALF,) + terms[0].shape[1:], jnp.bfloat16),
        in_specs=[smem] + [vmem] * len(terms),
        out_specs=vmem,
        compiler_params=pltpu.CompilerParams(vmem_limit_bytes=6 * 1024 * 1024),
    )(place, *terms)


def add(*terms):
    total = terms[0].astype(jnp.float32)
    for term in terms[1:]:
        total = total + term.astype(jnp.float32)
    return total.astype(jnp.bfloat16)


def finish_kernel(got, basis, spec_proj, rows, copies):
    n_freq = basis.shape[1] // 2
    blocks = n_freq // 128
    for p in range(TPO):
        turned = got[:, p].reshape(-1, TR).T
        rows[0, p] = turned
        spec_grad = jnp.dot(turned, basis[...], preferred_element_type=jnp.float32)
        both = spec_grad * spec_proj[p * TR : (p + 1) * TR]
        share = jnp.sum(both[:, :n_freq] + both[:, n_freq:], axis=0, keepdims=True)
        for n in range(blocks):
            block = jnp.broadcast_to(share[:, n * 128 : (n + 1) * 128], (copies.shape[0], 1, 128))
            copies[:, p * blocks + n : p * blocks + n + 1] = block


def finish(got, basis, spec_proj, n_ang):
    columns = basis.shape[0]
    vmem = pl.BlockSpec(memory_space=pltpu.VMEM)
    return pl.pallas_call(
        finish_kernel,
        out_shape=[
            jax.ShapeDtypeStruct((1, TPO, TR, columns), jnp.bfloat16),
            jax.ShapeDtypeStruct((n_ang, TPO * columns // 256, 128), jnp.float32),
        ],
        in_specs=[vmem] * 3,
        out_specs=[vmem] * 2,
        compiler_params=pltpu.CompilerParams(vmem_limit_bytes=12 * 1024 * 1024),
        cost_estimate=pl.CostEstimate(flops=10**9, bytes_accessed=10**6, transcendentals=0),
    )(got, basis, spec_proj)


def body(slab_views, footprint, row_shift, stretch, projections):
    n_grp = lax.axis_size("grp")
    n_ang = lax.axis_size("ang")
    chips = n_grp // 2
    owner = lax.axis_index("grp")
    chip, core = owner // 2, owner % 2
    views = slab_views[0]
    angles = views.shape[0]
    swap = [(i, i ^ 1) for i in range(n_grp)]
    onward = [(i, (i + (2 if i % 2 == 0 else -2)) % n_grp) for i in range(n_grp)]

    sibling_views = lax.ppermute(views, "grp", swap)
    place = jnp.stack([chip, core])
    meta = describe(footprint[0].T, row_shift, stretch)
    near, far = (meta, views), (lax.ppermute(meta, "grp", swap), sibling_views)
    known = (2, chips, place, [near, far])

    n_freq = n_ang * views.shape[1] // 2
    basis = jnp.asarray(dft_basis(2 * n_freq))
    spec_proj = jnp.dot(
        projections.reshape(-1, 2 * n_freq), basis, preferred_element_type=jnp.float32
    )

    early = units(0, 1, 2, chips, place, [near], fetched=True)[0]
    first = lax.ppermute(units(0, 1, 2, chips, place, [far], early)[0], "grp", onward)
    mine = units(1, 2, *known)
    second = lax.ppermute(mine[1], "grp", onward)
    kept = units(4, 2, 1, *known[1:])
    sending, kept, place = lax.optimization_barrier((add(first, mine[0]), kept, place))
    known = (2, chips, place, [near, far])
    first = lax.ppermute(sending, "grp", onward)
    mine = units(2, 2, *known)
    second = lax.ppermute(add(second, mine[1]), "grp", onward)
    first = lax.ppermute(add(first, mine[0]), "grp", onward)
    mine = units(3, 2, *known)
    second = lax.ppermute(add(second, mine[1]), "grp", onward)
    first = lax.ppermute(add(first, mine[0]), "grp", onward)
    to_first = lax.ppermute(second[1], "grp", swap)
    leaving, spec_proj = lax.optimization_barrier((first[1], spec_proj))
    to_second = lax.ppermute(leaving, "grp", swap)
    summed = close(place, first[0], to_first, kept[0][0], second[0], to_second, kept[1][0])

    got = lax.all_to_all(summed, "ang", split_axis=0, concat_axis=0, tiled=True)
    rows, copies = finish(got, basis, spec_proj, n_ang)
    shares = lax.all_to_all(copies, "ang", split_axis=0, concat_axis=0, tiled=True)
    filter_grad = (jnp.sum(shares, axis=0) * (1.0 / (2 * n_freq * angles))).reshape(TPO, 1, n_freq)
    return rows, filter_grad


def solution(mesh):
    return jax.shard_map(
        body,
        mesh=mesh,
        in_specs=(
            P("grp", None, "ang", None),
            P("grp", None, None),
            P("grp", None),
            P("grp", None),
            P("ang", None, "grp", None),
        ),
        out_specs=(P("ang", None, "grp", None), P(None, "grp", None)),
        check_vma=False,
    )
```

```python
import functools
import math

import jax
import jax.numpy as jnp
import numpy as np
from jax import lax
from jax.experimental import pallas as pl
from jax.experimental.pallas import tpu as pltpu
from jax.sharding import PartitionSpec as P

TR = 128
KF = 8
SZ = 1024
TPO = 2
WINDOW = 512
HALF = 16
BATCH = 8
FEW = KF // 2
UNROLL = 16
PIECE = 16


def dft_basis(columns):
    column_idx = np.arange(columns, dtype=np.int64)[:, None]
    freq_idx = np.arange(columns // 2, dtype=np.int64)[None, :]
    phases = ((column_idx * freq_idx) % columns).astype(np.float64) * (2.0 * math.pi / columns)
    return np.concatenate([np.cos(phases), np.sin(phases)], axis=1).astype(jnp.bfloat16)


def describe_kernel(lists, row_shift, stretch, meta, *held):
    held, arrived = held[:-1], held[-1]
    fetches = [
        pltpu.make_async_copy(source, target, arrived.at[n])
        for n, (source, target) in enumerate(zip((lists, row_shift, stretch), held))
    ]
    for fetch in fetches:
        fetch.start()
    for fetch in fetches:
        fetch.wait()
    count = jnp.sum((held[0][...] >= 0).astype(jnp.float32), axis=0, keepdims=True)
    meta[0:1] = held[0][0:1].astype(jnp.float32)
    meta[1:2] = count
    meta[2:3] = held[1][...]
    meta[3:4] = 1.0 / (TR * count * held[2][...] / SZ)


def describe(*operands):
    return pl.pallas_call(
        describe_kernel,
        out_shape=jax.ShapeDtypeStruct((4, operands[0].shape[1]), jnp.float32),
        in_specs=[pl.BlockSpec(memory_space=pltpu.HBM)] * 3,
        out_specs=pl.BlockSpec(memory_space=pltpu.VMEM),
        scratch_shapes=[pltpu.VMEM(operand.shape, operand.dtype) for operand in operands]
        + [pltpu.SemaphoreType.DMA((3,))],
        compiler_params=pltpu.CompilerParams(vmem_limit_bytes=1024 * 1024),
    )(*(pltpu.with_memory_space_constraint(operand, pltpu.HBM) for operand in operands))


def unit_kernel(hop, lanes, chips, slabs, resumed, fetched, place, *refs):
    sources = [refs[2 * s : 2 * s + 2] for s in range(slabs)]
    if fetched:
        refs, (brought, arrived) = refs[:-2], refs[-2:]
    outs, (total, listed) = refs[2 * slabs + resumed : -2], refs[-2:]
    angles = total.shape[1]
    chip, core = place[0], place[1]
    reach = chips // 2 - hop
    target = lax.rem(chip + jnp.where(core == 0, reach, -reach) + chips, chips)
    owners = 2 * chips
    row = lax.broadcasted_iota(jnp.int32, (PIECE, TR), 1).astype(jnp.float32)
    depth = lax.broadcasted_iota(jnp.int32, (PIECE, TR), 0)
    zero = jnp.zeros((PIECE, TR), jnp.bfloat16)
    owner = [(2 * target + (core ^ lane)).astype(jnp.float32) for lane in range(lanes)]
    first_angle = core * HALF
    size = angles * lanes + 1
    if fetched:
        fetch = pltpu.make_async_copy(sources[0][1].at[pl.ds(first_angle, HALF)], brought, arrived)
        fetch.start()
    total[...] = refs[2 * slabs][...] if resumed else jnp.zeros_like(total)

    def entry(meta, a, wanted):
        k = wanted - meta[0, a]
        k = jnp.where(k < 0.0, k + owners, k)
        return jnp.where(k < 0.0, k + owners, k)

    ends = []
    for s, (meta, _) in enumerate(sources):

        def note(i, found):
            a = (first_angle + i) & (2 * HALF - 1)
            count = meta[1, a]
            few = count < FEW + 1
            wide, narrow = found
            for lane in range(lanes):
                live = entry(meta, a, owner[lane]) < count
                listed[s, jnp.where(few, size - wide, narrow)] = i * lanes + lane
                wide = wide + jnp.where(live & few, 1, 0)
                narrow = narrow + jnp.where(live & ~few, 1, 0)
            return wide, narrow

        ends.append(
            lax.fori_loop(0, angles, note, (jnp.int32(0), jnp.int32(0)), unroll=UNROLL)
        )

    if fetched:
        fetch.wait()

    def add_tiles(window, batch, live, at_place):
        limits = [jnp.maximum(n - 1, 0) for n in live]

        def some(at, carry):
            for m in range(batch):
                for s, (meta, views) in enumerate(sources):
                    place = at * batch + m
                    n = listed[s, at_place(jnp.minimum(place, limits[s]))]
                    n = jnp.where(place < live[s], n, 0)
                    i, lane = n >> (lanes - 1), n & (lanes - 1)
                    a = (first_angle + i) & (2 * HALF - 1)
                    wanted = owner[0] if lanes == 1 else jnp.where(lane == 0, owner[0], owner[1])
                    k = entry(meta, a, wanted)
                    begin = (TR * k - meta[2, a]) * meta[3, a]
                    block = jnp.clip((begin - 1.0).astype(jnp.int32) >> 7, 0, (SZ - window) // 128)
                    start = jnp.where(
                        place < live[s], begin - (128 * block).astype(jnp.float32), -1e4
                    )
                    cycle = jnp.where(meta[0, a] + k >= owners, 1, 0)
                    centre = row * meta[3, a] + start
                    below = jnp.floor(centre)
                    above = centre - below
                    at_below = (1.0 - above).astype(jnp.bfloat16)
                    at_above = above.astype(jnp.bfloat16)
                    gap = (below.astype(jnp.int32) - depth).astype(jnp.int16)
                    pieces = []
                    for p in range(window // PIECE):
                        hit = jnp.where(gap == jnp.int16(p * PIECE - 1), at_above, zero)
                        pieces.append(jnp.where(gap == jnp.int16(p * PIECE), at_below, hit))
                    weights = jnp.concatenate(pieces, axis=0)
                    depths = pl.ds(pl.multiple_of(block * 128, 128), window)
                    view = brought[i, :, depths] if fetched else views[a, :, depths]
                    total[lane, i, cycle] += jnp.dot(
                        view, weights, preferred_element_type=jnp.float32
                    )
            return carry

        most = functools.reduce(jnp.maximum, live)
        lax.fori_loop(0, lax.div(most + batch - 1, batch), some, 0)

    add_tiles(WINDOW, BATCH // 4, [wide for wide, _ in ends], lambda n: size - n)
    add_tiles(WINDOW - 128, BATCH, [narrow for _, narrow in ends], lambda n: n)
    for half, out in enumerate(outs):
        out[...] = total[:, half * HALF : (half + 1) * HALF].astype(out.dtype)


def units(hop, halves, lanes, chips, place, sources, before=None, fetched=False):
    narrow = sources[0][1].shape[1]
    smem = pl.BlockSpec(memory_space=pltpu.SMEM)
    vmem = pl.BlockSpec(memory_space=pltpu.VMEM)
    shape = (lanes, HALF, TPO, narrow, TR)
    operands = [place] + [ref for source in sources for ref in source]
    specs = [smem] + [smem, pl.BlockSpec(memory_space=pltpu.HBM) if fetched else vmem] * len(sources)
    scratch = [
        pltpu.VMEM((lanes, halves * HALF) + shape[2:], jnp.float32),
        pltpu.SMEM((len(sources), halves * HALF * lanes + 2), jnp.int32),
    ]
    if fetched:
        operands[2] = pltpu.with_memory_space_constraint(operands[2], pltpu.HBM)
        scratch += [pltpu.VMEM((HALF,) + sources[0][1].shape[1:], jnp.bfloat16), pltpu.SemaphoreType.DMA]
    dtype = jnp.float32 if fetched else jnp.bfloat16
    if before is not None:
        operands, specs = operands + [before], specs + [vmem]
    return pl.pallas_call(
        functools.partial(
            unit_kernel, hop, lanes, chips, len(sources), before is not None, fetched
        ),
        out_shape=[jax.ShapeDtypeStruct(shape, dtype)] * halves,
        in_specs=specs,
        out_specs=[vmem] * halves,
        scratch_shapes=scratch,
        compiler_params=pltpu.CompilerParams(vmem_limit_bytes=12 * 1024 * 1024),
        cost_estimate=pl.CostEstimate(
            flops=12 * 10**8 * halves * len(sources), bytes_accessed=10**6, transcendentals=0
        ),
    )(*operands)


def close_kernel(place, here, there, mine, other_here, other_there, other_mine, out):
    core = place[1]
    for half, terms in enumerate(((here, there, mine), (other_here, other_there, other_mine))):
        total = sum(term[...].astype(jnp.float32) for term in terms)
        out[pl.ds((core ^ half) * HALF, HALF)] = total.astype(jnp.bfloat16)


def close(place, *terms):
    smem = pl.BlockSpec(memory_space=pltpu.SMEM)
    vmem = pl.BlockSpec(memory_space=pltpu.VMEM)
    return pl.pallas_call(
        close_kernel,
        out_shape=jax.ShapeDtypeStruct((2 * HALF,) + terms[0].shape[1:], jnp.bfloat16),
        in_specs=[smem] + [vmem] * len(terms),
        out_specs=vmem,
        compiler_params=pltpu.CompilerParams(vmem_limit_bytes=6 * 1024 * 1024),
    )(place, *terms)


def add(*terms):
    total = terms[0].astype(jnp.float32)
    for term in terms[1:]:
        total = total + term.astype(jnp.float32)
    return total.astype(jnp.bfloat16)


def finish_kernel(got, basis, spec_proj, rows, copies):
    n_freq = basis.shape[1] // 2
    blocks = n_freq // 128
    for p in range(TPO):
        turned = got[:, p].reshape(-1, TR).T
        rows[0, p] = turned
        spec_grad = jnp.dot(turned, basis[...], preferred_element_type=jnp.float32)
        both = spec_grad * spec_proj[p * TR : (p + 1) * TR]
        share = jnp.sum(both[:, :n_freq] + both[:, n_freq:], axis=0, keepdims=True)
        for n in range(blocks):
            block = jnp.broadcast_to(share[:, n * 128 : (n + 1) * 128], (copies.shape[0], 1, 128))
            copies[:, p * blocks + n : p * blocks + n + 1] = block


def finish(got, basis, spec_proj, n_ang):
    columns = basis.shape[0]
    vmem = pl.BlockSpec(memory_space=pltpu.VMEM)
    return pl.pallas_call(
        finish_kernel,
        out_shape=[
            jax.ShapeDtypeStruct((1, TPO, TR, columns), jnp.bfloat16),
            jax.ShapeDtypeStruct((n_ang, TPO * columns // 256, 128), jnp.float32),
        ],
        in_specs=[vmem] * 3,
        out_specs=[vmem] * 2,
        compiler_params=pltpu.CompilerParams(vmem_limit_bytes=12 * 1024 * 1024),
        cost_estimate=pl.CostEstimate(flops=10**9, bytes_accessed=10**6, transcendentals=0),
    )(got, basis, spec_proj)


def body(slab_views, footprint, row_shift, stretch, projections):
    n_grp = lax.axis_size("grp")
    n_ang = lax.axis_size("ang")
    chips = n_grp // 2
    owner = lax.axis_index("grp")
    chip, core = owner // 2, owner % 2
    views = slab_views[0]
    angles = views.shape[0]
    swap = [(i, i ^ 1) for i in range(n_grp)]
    onward = [(i, (i + (2 if i % 2 == 0 else -2)) % n_grp) for i in range(n_grp)]

    sibling_views = lax.ppermute(views, "grp", swap)
    place = jnp.stack([chip, core])
    meta = describe(footprint[0].T, row_shift, stretch)
    near, far = (meta, views), (lax.ppermute(meta, "grp", swap), sibling_views)
    known = (2, chips, place, [near, far])

    n_freq = n_ang * views.shape[1] // 2
    basis = jnp.asarray(dft_basis(2 * n_freq))
    spec_proj = jnp.dot(
        projections.reshape(-1, 2 * n_freq), basis, preferred_element_type=jnp.float32
    )

    early = units(0, 1, 2, chips, place, [near], fetched=True)[0]
    first = lax.ppermute(units(0, 1, 2, chips, place, [far], early)[0], "grp", onward)
    mine = units(1, 2, *known)
    second = lax.ppermute(mine[1], "grp", onward)
    kept = units(4, 2, 1, *known[1:])
    sending, kept, place = lax.optimization_barrier((add(first, mine[0]), kept, place))
    known = (2, chips, place, [near, far])
    first = lax.ppermute(sending, "grp", onward)
    mine = units(2, 2, *known)
    second = lax.ppermute(add(second, mine[1]), "grp", onward)
    first = lax.ppermute(add(first, mine[0]), "grp", onward)
    mine = units(3, 2, *known)
    second = lax.ppermute(add(second, mine[1]), "grp", onward)
    first = lax.ppermute(add(first, mine[0]), "grp", onward)
    to_first = lax.ppermute(second[1], "grp", swap)
    leaving, spec_proj = lax.optimization_barrier((first[1], spec_proj))
    to_second = lax.ppermute(leaving, "grp", swap)
    summed = close(place, first[0], to_first, kept[0][0], second[0], to_second, kept[1][0])

    got = lax.all_to_all(summed, "ang", split_axis=0, concat_axis=0, tiled=True)
    rows, copies = finish(got, basis, spec_proj, n_ang)
    shares = lax.all_to_all(copies, "ang", split_axis=0, concat_axis=0, tiled=True)
    filter_grad = (jnp.sum(shares, axis=0) * (1.0 / (2 * n_freq * angles))).reshape(TPO, 1, n_freq)
    return rows, filter_grad


def solution(mesh):
    return jax.shard_map(
        body,
        mesh=mesh,
        in_specs=(
            P("grp", None, "ang", None),
            P("grp", None, None),
            P("grp", None),
            P("grp", None),
            P("ang", None, "grp", None),
        ),
        out_specs=(P("ang", None, "grp", None), P(None, "grp", None)),
        check_vma=False,
    )
```
